32 devices in a mesh: seq: 16 (over z, y, core), tp: 2 (over x).
Axes of the slice: x: 2, y: 2, z: 4, core: 2. Of those that a mesh axis runs over, the one named last changes fastest.
Arguments:
- queries: bfloat16 [4096, 5120], P('seq', 'tp'), may hold values from -120 to 120, as said below
- prompt_keys: bfloat16 [2048, 1024], P('seq', 'tp'), may hold values from -4 to 4
- prompt_values: bfloat16 [2048, 1024], P('seq', 'tp'), may hold values from -6 to 6
- response_keys: bfloat16 [4096, 1024], P('seq', 'tp'), may hold values from -6 to 6
- response_values: bfloat16 [4096, 1024], P('seq', 'tp'), may hold values from -6 to 6
- lengths: int32 [16], replicated, may hold values from 1 to 2048, 4096 in all
- out_weight: bfloat16 [5120, 5120], P('tp'), may hold values from -0.125 to 0.125
Outputs:
- projected: bfloat16 [4096, 5120], P('seq', 'tp')
The draws below stay inside these ranges and needn't reach their ends.
Inputs may be any that keep to these rules, and one draw needn't show every extreme that they name: `queries`: in a few rows a query head may be a multiple of a prompt key of its key head. 16 lengths that sum to 4096; the longest has exactly 2048 tokens.
All inputs are finite; a program needn't handle non-finite values.
Results may differ from the reference program's by a relative error of at most 0.014.
Values may be sent and summed in bfloat16 or wider, within the bound.
No kernel may reach another device: no remote copies, remote signals or barrier semaphores. Data moves between devices by JAX's collectives and lax.ppermute only.
A program may use at most 192 MiB of HBM per device.

```python
import math
import jax
import jax.numpy as jnp
import numpy as np
from jax import lax

D = 5120
HEADS = 40
KVH = 8
HD = 128
N_RESP = 16
PROMPT = 2048
RESP = 4096
MOST = 2048
N_TP = 2


def prompt_key_base(key):
    drawn = jax.random.normal(jax.random.fold_in(key, 11), (PROMPT, KVH * HD), jnp.float32)
    return jnp.clip(drawn, -4.0, 4.0)


def draw_prompt_keys(key, part):
    return prompt_key_base(key).astype(jnp.bfloat16)


def draw_queries(key, part):
    drawn = jax.random.normal(jax.random.fold_in(key, 12), (RESP, HEADS * HD), jnp.float32)
    return drawn.astype(jnp.bfloat16)


def strengthened(entries, key, source, target, shards_of, factor):
    def block_of(axis_at):
        return (jnp.arange(entries.shape[axis_at]) // (entries.shape[axis_at] // shards_of)).reshape((-1,) + (1,) * (entries.ndim - 1 - axis_at))

    first = jax.random.permutation(key, shards_of)[block_of(target)]
    far = (block_of(target) + shards_of // 2) % shards_of
    return jnp.where((block_of(source) == first) | (block_of(source) == far), factor * entries, entries)


def block_scale(stream_key, shape, shards, least, top_value):
    factor_of = 1.0
    for dim, parts in shards:
        draws = jax.random.uniform(jax.random.fold_in(jax.random.fold_in(stream_key, 6), dim), (parts,), jnp.float32, least / len(shards), top_value / len(shards))
        factor_of = factor_of * jnp.repeat(jnp.exp(draws), shape[dim] // parts).reshape((-1,) + (1,) * (len(shape) - 1 - dim))
    return factor_of


def length_profile(count, total, bound, skew):
    weights = [(1 << 20) // math.isqrt(rank ** skew) + 1 for rank in range(2, count + 1)]
    spare, holding = total - bound - (count - 1), [1] * (count - 1)
    while spare > 0:
        free = [i for i in range(count - 1) if holding[i] < bound]
        pool, remaining = sum([weights[i] for i in free]), spare
        for i in free:
            addition = min(bound - holding[i], max(1, remaining * weights[i] // pool), spare)
            holding[i] = holding[i] + addition
            spare = spare - addition
    return np.array([bound] + holding)


def ragged_sizes(rng, amount, total, reach, skew):
    if amount == 2:
        one = jax.random.randint(rng, (), max(1, total - reach), min(reach, total - 1) + 1)
        return jnp.stack([one, total - one])
    sizes = jnp.asarray(length_profile(amount, total, reach, skew), jnp.int32)
    couples = (amount - 1) // 2
    source_of, taker = sizes[1:1 + 2 * couples:2], sizes[2:2 + 2 * couples:2]
    slack = jnp.minimum(source_of - 1, reach - taker)
    shifted = jax.random.randint(jax.random.fold_in(rng, 1), (couples,), 0, 1 << 20) % (slack + 1)
    sizes = sizes.at[1:1 + 2 * couples:2].set(source_of - shifted).at[2:2 + 2 * couples:2].set(taker + shifted)
    return sizes[jax.random.permutation(jax.random.fold_in(rng, 2), amount)]


def normal_values(own_key, shape, width, most, split=(), held_as=jnp.bfloat16):
    loudness = block_scale(own_key, shape, split, -0.22, 0.18) if split else 1.0
    values = jax.random.normal(own_key, shape, jnp.float32) * width * loudness
    return jnp.minimum(jnp.maximum(values, -most), most).astype(held_as)


def heavy_noise(key, shape, deviation, limit, cuts, heavy, held_as=jnp.bfloat16):
    result = deviation * jax.random.normal(key, shape, jnp.float32)
    if cuts:
        result = result * block_scale(key, shape, cuts, -0.22, 0.18)
    return jnp.clip(strengthened(result, jax.random.fold_in(key, 3), *heavy), -limit, limit).astype(held_as)


def setup_inputs(seed: int = 0) -> dict:
    keys = jax.random.split(jax.random.key(seed), 8)
    queries = draw_queries(jax.random.fold_in(keys[7], 71), 0)
    prompt_keys = draw_prompt_keys(jax.random.fold_in(keys[7], 71), 0)
    prompt_values = normal_values(keys[2], (PROMPT, KVH * HD), 1.0, 6.0, ((0, 16), (1, 2)))
    response_keys = normal_values(keys[3], (RESP, KVH * HD), 1.0, 6.0, ((0, 16), (1, 2)))
    response_values = normal_values(keys[4], (RESP, KVH * HD), 1.0, 6.0, ((0, 16), (1, 2)))
    lengths = ragged_sizes(keys[5], N_RESP, RESP, MOST, 2).astype(jnp.int32)
    out_weight = heavy_noise(keys[6], (HEADS * HD, D), (HEADS * HD) ** -0.5, 0.125, ((0, 2),), (0, 1, 2, 2.0))
    return dict(queries=queries, prompt_keys=prompt_keys, prompt_values=prompt_values, response_keys=response_keys, response_values=response_values, lengths=lengths, out_weight=out_weight)


def segment_layout(lengths):
    positions = jnp.arange(RESP, dtype=jnp.int32)
    seg_ends = jnp.cumsum(lengths).astype(jnp.int32)
    seg_starts = seg_ends - lengths
    inside = (positions[:, None] >= seg_starts[None, :]) & (positions[:, None] < seg_ends[None, :])
    own_start = jnp.sum(jnp.where(inside, seg_starts[None, :], 0), axis=1).astype(jnp.int32)
    return positions, own_start


def reference(queries, prompt_keys, prompt_values, response_keys, response_values, lengths, out_weight):
    group_size = HEADS // KVH
    block_rows = math.gcd(RESP, 128)
    window = min(MOST + block_rows, RESP)
    scale_factor = HD ** -0.5
    positions, own_start = segment_layout(lengths)
    prompt_k = prompt_keys.astype(jnp.float32).reshape(PROMPT, KVH, HD)
    prompt_v = prompt_values.astype(jnp.float32).reshape(PROMPT, KVH, HD)

    def one_block(index):
        first_row = (index * block_rows).astype(jnp.int32)
        query_block = lax.dynamic_slice_in_dim(queries, first_row, block_rows, 0)
        query_block = query_block.astype(jnp.float32).reshape(block_rows, KVH, group_size, HD)
        query_pos = lax.dynamic_slice_in_dim(positions, first_row, block_rows, 0)
        query_first = lax.dynamic_slice_in_dim(own_start, first_row, block_rows, 0)
        begin = jnp.clip(first_row + block_rows - window, 0, RESP - window).astype(jnp.int32)
        resp_k = lax.dynamic_slice_in_dim(response_keys, begin, window, 0).astype(jnp.float32).reshape(window, KVH, HD)
        resp_v = lax.dynamic_slice_in_dim(response_values, begin, window, 0).astype(jnp.float32).reshape(window, KVH, HD)
        key_pos = begin + jnp.arange(window, dtype=jnp.int32)
        visible = (key_pos[None, :] <= query_pos[:, None]) & (key_pos[None, :] >= query_first[:, None])
        prompt_scores = jnp.einsum("rkgd,nkd->rkgn", query_block, prompt_k) * scale_factor
        resp_scores = jnp.einsum("rkgd,nkd->rkgn", query_block, resp_k) * scale_factor
        resp_scores = jnp.where(visible[:, None, None, :], resp_scores, -jnp.inf)
        scores = jnp.concatenate([prompt_scores, resp_scores], axis=3)
        top = jnp.max(scores, axis=3)
        weights = jnp.exp(scores - top[..., None])
        summed = jnp.sum(weights, axis=3)
        rounded = lax.optimization_barrier(weights.astype(jnp.bfloat16)).astype(jnp.float32)
        all_values = jnp.concatenate([prompt_v, resp_v], axis=0)
        numer = jnp.einsum("rkgn,nkd->rkgd", rounded, all_values)
        return (numer / summed[..., None]).astype(jnp.bfloat16).reshape(block_rows, HEADS * HD)

    attended = lax.map(one_block, jnp.arange(RESP // block_rows, dtype=jnp.int32))
    attended = attended.reshape(RESP, HEADS * HD)
    group_cols = HEADS * HD // N_TP
    total = jnp.zeros((RESP, D), jnp.float32)
    for group in range(N_TP):
        cols = attended[:, group * group_cols:(group + 1) * group_cols]
        rows = out_weight[group * group_cols:(group + 1) * group_cols, :]
        partial_term = jnp.dot(cols, rows, preferred_element_type=jnp.float32).astype(jnp.bfloat16)
        total = total + partial_term.astype(jnp.float32)
    return total.astype(jnp.bfloat16)
```

```python
import functools

import jax
import jax.numpy as jnp
from jax import lax
from jax.experimental import pallas as pl
from jax.experimental.pallas import tpu as pltpu
from jax.sharding import PartitionSpec as P

HEADS = 40
KVH = 8
HD = 128
GROUP = HEADS // KVH
WIDE = GROUP * HD
LOG2E = 1.4426950408889634
LOW = -1e30
PARAMS = dict(vmem_limit_bytes=48 * 2**20)


def segment_layout(lengths, first_row, row_count):
    positions = first_row + jnp.arange(row_count, dtype=jnp.int32)
    seg_ends = jnp.cumsum(lengths)
    seg_starts = seg_ends - lengths
    inside = (positions[:, None] >= seg_starts[None, :]) & (positions[:, None] < seg_ends[None, :])
    own_start = jnp.sum(jnp.where(inside, seg_starts[None, :], 0), axis=1)
    return (positions, own_start)


def update_state(running, grouped, key_block, value_block, visible, scale_factor):
    maximum, summed, weighted = running
    scores = (
        jnp.einsum("rkgd,nkd->rkgn", grouped, key_block, preferred_element_type=jnp.float32)
        * scale_factor
    )
    if visible is not None:
        scores = jnp.where(visible[:, None, None, :], scores, -jnp.inf)
    new_max = jnp.maximum(maximum, jnp.max(scores, axis=3))
    weights = jnp.exp(scores - new_max[..., None])
    rescale = jnp.exp(maximum - new_max)
    rounded = weights.astype(jnp.bfloat16)
    summed = summed * rescale + jnp.sum(weights, axis=3)
    weighted = weighted * rescale[..., None] + jnp.einsum(
        "rkgn,nkd->rkgd", rounded, value_block, preferred_element_type=jnp.float32
    )
    return (new_max, summed, weighted)


def per_device_general(
    queries, prompt_keys, prompt_values, response_keys, response_values, lengths, out_weight
):
    row_count = queries.shape[0]
    kv_local = prompt_keys.shape[1] // HD
    scale_factor = HD ** (-0.5)
    grouped = queries.reshape(row_count, kv_local, GROUP, HD)
    first_row = lax.axis_index("seq") * row_count
    positions, own_start = segment_layout(lengths, first_row, row_count)
    softmax_state = (
        jnp.full((row_count, kv_local, GROUP), -jnp.inf, jnp.float32),
        jnp.zeros((row_count, kv_local, GROUP), jnp.float32),
        jnp.zeros((row_count, kv_local, GROUP, HD), jnp.float32),
    )
    prompt_pair = jnp.stack([prompt_keys, prompt_values])
    fragment = lax.all_gather(prompt_pair, "seq", axis=1, tiled=True)
    frag_rows = fragment.shape[1]
    key_block = fragment[0].reshape(frag_rows, kv_local, HD)
    value_block = fragment[1].reshape(frag_rows, kv_local, HD)
    softmax_state = update_state(softmax_state, grouped, key_block, value_block, None, scale_factor)
    response_pair = jnp.stack([response_keys, response_values])
    fragment = lax.all_gather(response_pair, "seq", axis=1, tiled=True)
    frag_rows = fragment.shape[1]
    key_pos = jnp.arange(frag_rows, dtype=jnp.int32)
    visible = (key_pos[None, :] <= positions[:, None]) & (key_pos[None, :] >= own_start[:, None])
    key_block = fragment[0].reshape(frag_rows, kv_local, HD)
    value_block = fragment[1].reshape(frag_rows, kv_local, HD)
    softmax_state = update_state(
        softmax_state, grouped, key_block, value_block, visible, scale_factor
    )
    maximum, summed, weighted = softmax_state
    attended = (
        (weighted / summed[..., None])
        .astype(jnp.bfloat16)
        .reshape(row_count, kv_local * GROUP * HD)
    )
    partial_out = jnp.dot(attended, out_weight, preferred_element_type=jnp.float32)
    return lax.psum_scatter(partial_out.astype(jnp.bfloat16), "tp", scatter_dimension=1, tiled=True)


def pack_kernel(meta, *refs):
    count = len(refs) // 2
    for source, target in zip(refs[:count], refs[count:]):
        target[...] = source[...]


def pack_call(meta, arrays, width, group):
    in_specs, out_specs, out_shape, operands = [], [], [], []
    for array in arrays:
        rows = array.shape[0]
        for d in range(group):
            in_specs.append(
                pl.BlockSpec((rows, width), lambda i, meta, d=d: (0, meta[0] ^ d))
            )
            out_specs.append(pl.BlockSpec((rows, width), lambda i, meta: (0, 0)))
            out_shape.append(jax.ShapeDtypeStruct((rows, width), array.dtype))
            operands.append(array)
    return pl.pallas_call(
        pack_kernel,
        grid_spec=pltpu.PrefetchScalarGridSpec(
            num_scalar_prefetch=1, grid=(1,), in_specs=in_specs, out_specs=out_specs
        ),
        out_shape=out_shape,
        compiler_params=pltpu.CompilerParams(**PARAMS),
        name="pack",
    )(meta, *operands)


def pack_kv_kernel(meta, *refs):
    group = len(refs) // 3
    for d in range(group):
        keys, values, target = refs[2 * d], refs[2 * d + 1], refs[2 * group + d]
        target[:, :HD] = keys[...]
        target[:, HD:] = values[...]


def pack_kv_call(meta, keys, values, group):
    rows = keys.shape[0]
    in_specs, operands = [], []
    for d in range(group):
        for array in (keys, values):
            in_specs.append(pl.BlockSpec((rows, HD), lambda i, meta, d=d: (0, meta[0] ^ d)))
            operands.append(array)
    return pl.pallas_call(
        pack_kv_kernel,
        grid_spec=pltpu.PrefetchScalarGridSpec(
            num_scalar_prefetch=1,
            grid=(1,),
            in_specs=in_specs,
            out_specs=[pl.BlockSpec((rows, 2 * HD), lambda i, meta: (0, 0))] * group,
        ),
        out_shape=[jax.ShapeDtypeStruct((rows, 2 * HD), keys.dtype)] * group,
        compiler_params=pltpu.CompilerParams(**PARAMS),
        name="pack_kv",
    )(meta, *operands)


def join_kernel(*refs):
    rows = refs[0].shape[0]
    for d, source in enumerate(refs[:-1]):
        refs[-1][d * rows : (d + 1) * rows, :] = source[...]


def join_call(parts):
    rows, width = parts[0].shape
    return pl.pallas_call(
        join_kernel,
        out_shape=jax.ShapeDtypeStruct((rows * len(parts), width), parts[0].dtype),
        compiler_params=pltpu.CompilerParams(**PARAMS),
        name="join",
    )(*parts)


def attend_kernel(
    meta, lengths, *refs, kinds, group, rows, offset, has_state, final, n_lengths, scale
):
    refs = list(refs)
    q_ref = refs.pop(0)
    kv_refs = [refs.pop(0) for _ in kinds]
    if has_state:
        acc_in, stat_in = refs.pop(0), refs.pop(0)
    if final:
        out_ref = refs.pop(0)
    else:
        acc_out, stat_out = refs.pop(0), refs.pop(0)
    acc_ref, max_ref = refs
    block = pl.program_id(0) + offset
    row_base = (meta[1] * group + (meta[0] ^ block)) * rows
    lane = lax.broadcasted_iota(jnp.int32, (rows, HD), 1)

    if has_state:
        stats = stat_in[...]
        for h in range(GROUP):
            acc_ref[h, :, :HD] = acc_in[:, h * HD : (h + 1) * HD]
            acc_ref[h, :, HD:] = jnp.broadcast_to(stats[:, 8 + h : 9 + h], (rows, HD))
            max_ref[h] = jnp.broadcast_to(stats[:, h : h + 1], (rows, HD))

    def update(h, keys, wide_values, visible, fresh):
        q = q_ref[:, h * HD : (h + 1) * HD]
        s = lax.dot_general(
            q, keys, (((1,), (1,)), ((), ())), preferred_element_type=jnp.float32
        )
        if visible is not None:
            s = jnp.where(visible, s, LOW)
        top = jnp.max(s, axis=1, keepdims=True)
        if not fresh:
            old = max_ref[h][:, :1]
            top = jnp.maximum(old, top)
        p = jnp.exp2((s - top) * scale).astype(jnp.bfloat16)
        part = jnp.dot(p, wide_values, preferred_element_type=jnp.float32)
        if not fresh:
            part = acc_ref[h] * jnp.exp2((old - top) * scale) + part
        acc_ref[h] = part
        max_ref[h] = jnp.broadcast_to(top, (rows, HD))

    fresh = not has_state
    for kind, kv_ref in zip(kinds, kv_refs):
        if kind is None:
            total = kv_ref.shape[0]
            step = 512 if total % 512 == 0 else total
            for c in range(total // step):
                keys = kv_ref[c * step : (c + 1) * step, :HD]
                values = kv_ref[c * step : (c + 1) * step, HD:]
                wide = jnp.concatenate([values, jnp.ones_like(values)], axis=1)
                for h in range(GROUP):
                    update(h, keys, wide, None, fresh)
                fresh = False
            continue

        def first_of(position):
            start, found = jnp.int32(0), jnp.int32(0)
            for r in range(n_lengths):
                found = jnp.where(start <= position, start, found)
                start = start + lengths[r]
            return found

        first_low = first_of(row_base)
        first_high = first_of(row_base + rows - 1)

        def one_block(j, carry, kind=kind, kv_ref=kv_ref, first_low=first_low, first_high=first_high):
            key_base = ((meta[1] - kind) * group + (meta[0] ^ j)) * rows
            needed = (key_base <= row_base + rows - 1) & (key_base + rows - 1 >= first_low)
            whole = (key_base + rows - 1 <= row_base) & (key_base >= first_high)
            at = pl.ds(pl.multiple_of(j * rows, rows), rows)

            def run(visible):
                keys = kv_ref[at, :HD]
                values = kv_ref[at, HD:]
                wide = jnp.concatenate([values, jnp.ones_like(values)], axis=1)
                for h in range(GROUP):
                    update(h, keys, wide, visible, False)

            @pl.when(needed & whole)
            def _():
                run(None)

            @pl.when(needed & jnp.logical_not(whole))
            def _():
                position = row_base + lax.broadcasted_iota(jnp.int32, (rows, 1), 0)
                first = jnp.zeros((rows, 1), jnp.int32)
                start = jnp.int32(0)
                for r in range(n_lengths):
                    first = jnp.where(start <= position, start, first)
                    start = start + lengths[r]
                key_pos = key_base + lax.broadcasted_iota(jnp.int32, (rows, rows), 1)
                run((key_pos >= first) & (key_pos <= position))

            return carry

        lax.fori_loop(0, group, one_block, 0)

    if final:
        for h in range(GROUP):
            out_ref[:, h * HD : (h + 1) * HD] = (
                acc_ref[h, :, :HD] / acc_ref[h, :, HD:]
            ).astype(jnp.bfloat16)
    else:
        stats = jnp.zeros((rows, HD), jnp.float32)
        for h in range(GROUP):
            acc_out[:, h * HD : (h + 1) * HD] = acc_ref[h, :, :HD]
            stats = jnp.where(lane == h, max_ref[h], stats)
            stats = jnp.where(lane == 8 + h, acc_ref[h, :, HD:], stats)
        stat_out[...] = stats


def attend_call(meta, lengths, q, pieces, state, final, group, rows, offset):
    kinds = tuple(kind for kind, _ in pieces)
    arrays = [array for _, array in pieces]
    count = q.shape[0] // rows
    row_spec = pl.BlockSpec((rows, WIDE), lambda i, *_: (i, 0))
    stat_spec = pl.BlockSpec((rows, HD), lambda i, *_: (i, 0))
    in_specs = [row_spec] + [pl.BlockSpec(a.shape, lambda i, *_: (0, 0)) for a in arrays]
    operands = [q] + arrays
    if state is not None:
        in_specs += [row_spec, stat_spec]
        operands += list(state)
    if final:
        out_specs = [row_spec]
        out_shape = [jax.ShapeDtypeStruct(q.shape, jnp.bfloat16)]
    else:
        out_specs = [row_spec, stat_spec]
        out_shape = [
            jax.ShapeDtypeStruct(q.shape, jnp.float32),
            jax.ShapeDtypeStruct((q.shape[0], HD), jnp.float32),
        ]
    keys = sum(a.shape[0] for a in arrays)
    elements = q.shape[0] * GROUP * keys
    return pl.pallas_call(
        functools.partial(
            attend_kernel,
            kinds=kinds,
            group=group,
            rows=rows,
            offset=offset,
            has_state=state is not None,
            final=final,
            n_lengths=lengths.shape[0],
            scale=HD**-0.5 * LOG2E,
        ),
        grid_spec=pltpu.PrefetchScalarGridSpec(
            num_scalar_prefetch=2,
            grid=(count,),
            in_specs=in_specs,
            out_specs=out_specs,
            scratch_shapes=[
                pltpu.VMEM((GROUP, rows, 2 * HD), jnp.float32),
                pltpu.VMEM((GROUP, rows, HD), jnp.float32),
            ],
        ),
        out_shape=out_shape,
        compiler_params=pltpu.CompilerParams(**PARAMS),
        cost_estimate=pl.CostEstimate(
            flops=elements * HD * 8, bytes_accessed=4 * q.size, transcendentals=elements
        ),
        name="attend",
    )(meta, lengths, *operands)


def project_kernel(meta, *refs, group):
    parts, weight, out = refs[:group], refs[group], refs[group + 1]
    total = None
    for d in range(group):
        at = pl.ds(pl.multiple_of((meta[0] ^ d) * WIDE, WIDE), WIDE)
        term = jnp.dot(parts[d][...], weight[at, :], preferred_element_type=jnp.float32)
        total = term if total is None else total + term
    out[...] = total.astype(jnp.bfloat16)


def project_call(meta, parts, weight, first_tile, tiles, tile):
    group = len(parts)
    rows = parts[0].shape[0]
    depth = weight.shape[0]
    return pl.pallas_call(
        functools.partial(project_kernel, group=group),
        grid_spec=pltpu.PrefetchScalarGridSpec(
            num_scalar_prefetch=1,
            grid=(tiles,),
            in_specs=[pl.BlockSpec((rows, WIDE), lambda i, meta: (0, 0))] * group
            + [pl.BlockSpec((depth, tile), lambda i, meta: (0, meta[2] + first_tile + i))],
            out_specs=pl.BlockSpec((rows, tile), lambda i, meta: (0, i)),
        ),
        out_shape=jax.ShapeDtypeStruct((rows, tiles * tile), jnp.bfloat16),
        compiler_params=pltpu.CompilerParams(**PARAMS),
        cost_estimate=pl.CostEstimate(
            flops=2 * rows * depth * tiles * tile,
            bytes_accessed=2 * depth * tiles * tile,
            transcendentals=0,
        ),
        name="project",
    )(meta, *parts, weight)


def sum_kernel(*refs, tile):
    own, parts, out = refs[0], refs[1:-1], refs[-1]
    for c, part in enumerate(parts):
        at = slice(c * tile, (c + 1) * tile)
        out[:, at] = (own[:, at].astype(jnp.float32) + part[...].astype(jnp.float32)).astype(
            jnp.bfloat16
        )


def sum_call(own, parts, tile):
    return pl.pallas_call(
        functools.partial(sum_kernel, tile=tile),
        out_shape=jax.ShapeDtypeStruct(own.shape, jnp.bfloat16),
        compiler_params=pltpu.CompilerParams(**PARAMS),
        name="sum",
    )(own, *parts)


def per_device_planes(
    queries,
    prompt_keys,
    prompt_values,
    response_keys,
    response_values,
    lengths,
    out_weight,
    *,
    n_seq,
    n_tp,
):
    rows = queries.shape[0]
    group = prompt_keys.shape[1] // HD
    levels = n_seq // group
    seq = lax.axis_index("seq")
    me = lax.rem(seq, group)
    level = lax.div(seq, group)
    tp = lax.axis_index("tp")
    half = out_weight.shape[1] // n_tp
    tile = 512
    chunks = half // tile
    meta = jnp.stack([me, level, (1 - tp) * chunks, tp * chunks]).astype(jnp.int32)
    meta_own = jnp.stack([me, level, tp * chunks, tp * chunks]).astype(jnp.int32)

    def swap(x, d):
        return lax.ppermute(
            x, "seq", [(i, i - i % group + ((i % group) ^ d)) for i in range(n_seq)]
        )

    def shift(x, k, around):
        pairs = [(i, i + k * group) for i in range(n_seq)]
        if around:
            pairs = [(i, j % n_seq) for i, j in pairs]
        return lax.ppermute(x, "seq", [(i, j) for i, j in pairs if 0 <= j < n_seq])

    packed_p = pack_kv_call(meta, prompt_keys, prompt_values, group)
    packed_r = pack_kv_call(meta, response_keys, response_values, group)
    packed_q = pack_call(meta, [queries], WIDE, group)
    got_p = [packed_p[0]] + [swap(packed_p[d], d) for d in range(1, group)]
    got_r = [packed_r[0]] + [swap(packed_r[d], d) for d in range(1, group)]
    got_q = [packed_q[0]] + [swap(packed_q[d], d) for d in range(1, group)]
    prompt = join_call(got_p)
    response = join_call(got_r)
    q_near = join_call(got_q[:2])
    q_far = join_call(got_q[2:])
    others = [shift(prompt, k, True) for k in range(1, levels)]
    back1 = shift(response, 1, False)
    back2 = shift(back1, 1, False)

    def attend(q, offset, pieces, state, final):
        return attend_call(meta, lengths, q, pieces, state, final, group, rows, offset)

    near = attend(q_near, 0, [(None, prompt), (0, response)], None, False)
    far = attend(q_far, 2, [(None, prompt), (0, response)], None, False)
    rest = [(None, other) for other in others] + [(1, back1)]
    far = attend(q_far, 2, rest, far, False)
    near = attend(q_near, 0, rest, near, False)
    (far,) = attend(q_far, 2, [(2, back2)], far, True)
    (near,) = attend(q_near, 0, [(2, back2)], near, True)
    done = [near[:rows], near[rows:], far[:rows], far[rows:]]
    parts = [done[0]] + [swap(done[d], d) for d in range(1, group)]

    got = []
    for c in range(chunks):
        got.append(
            lax.ppermute(
                project_call(meta, parts, out_weight, c, 1, tile), "tp", [(0, 1), (1, 0)]
            )
        )
    own = project_call(meta_own, parts, out_weight, 0, chunks, tile)
    return sum_call(own, got, tile)


def solution(mesh):
    in_specs = (
        P("seq", "tp"),
        P("seq", "tp"),
        P("seq", "tp"),
        P("seq", "tp"),
        P("seq", "tp"),
        P(),
        P("tp", None),
    )
    out_specs = P("seq", "tp")
    n_seq, n_tp = mesh.shape["seq"], mesh.shape["tp"]
    if n_tp == 2 and n_seq == 16:
        body = functools.partial(per_device_planes, n_seq=n_seq, n_tp=n_tp)
    else:
        body = per_device_general
    return jax.shard_map(body, mesh=mesh, in_specs=in_specs, out_specs=out_specs, check_vma=False)
```

```python
import functools

import jax
import jax.numpy as jnp
from jax import lax
from jax.experimental import pallas as pl
from jax.experimental.pallas import tpu as pltpu
from jax.sharding import PartitionSpec as P

HEADS = 40
KVH = 8
HD = 128
GROUP = HEADS // KVH
WIDE = GROUP * HD
LOG2E = 1.4426950408889634
LOW = -1e30
PIECES = 2
TILE = 256
VMEM = pl.BlockSpec(memory_space=pltpu.VMEM)
SMEM = pl.BlockSpec(memory_space=pltpu.SMEM)
SMALL = pl.CostEstimate(flops=1000, bytes_accessed=1000, transcendentals=0)
LARGE = pl.CostEstimate(flops=2 * 10**10, bytes_accessed=1000, transcendentals=0)
PARAMS = dict(vmem_limit_bytes=16 * 2**20)


def segment_layout(lengths, first_row, row_count):
    positions = first_row + jnp.arange(row_count, dtype=jnp.int32)
    seg_ends = jnp.cumsum(lengths)
    seg_starts = seg_ends - lengths
    inside = (positions[:, None] >= seg_starts[None, :]) & (positions[:, None] < seg_ends[None, :])
    own_start = jnp.sum(jnp.where(inside, seg_starts[None, :], 0), axis=1)
    return (positions, own_start)


def update_state(running, grouped, key_block, value_block, visible, scale_factor):
    maximum, summed, weighted = running
    scores = (
        jnp.einsum("rkgd,nkd->rkgn", grouped, key_block, preferred_element_type=jnp.float32)
        * scale_factor
    )
    if visible is not None:
        scores = jnp.where(visible[:, None, None, :], scores, -jnp.inf)
    new_max = jnp.maximum(maximum, jnp.max(scores, axis=3))
    weights = jnp.exp(scores - new_max[..., None])
    rescale = jnp.exp(maximum - new_max)
    rounded = weights.astype(jnp.bfloat16)
    summed = summed * rescale + jnp.sum(weights, axis=3)
    weighted = weighted * rescale[..., None] + jnp.einsum(
        "rkgn,nkd->rkgd", rounded, value_block, preferred_element_type=jnp.float32
    )
    return (new_max, summed, weighted)


def per_device_general(
    queries, prompt_keys, prompt_values, response_keys, response_values, lengths, out_weight
):
    row_count = queries.shape[0]
    kv_local = prompt_keys.shape[1] // HD
    scale_factor = HD ** (-0.5)
    grouped = queries.reshape(row_count, kv_local, GROUP, HD)
    first_row = lax.axis_index("seq") * row_count
    positions, own_start = segment_layout(lengths, first_row, row_count)
    softmax_state = (
        jnp.full((row_count, kv_local, GROUP), -jnp.inf, jnp.float32),
        jnp.zeros((row_count, kv_local, GROUP), jnp.float32),
        jnp.zeros((row_count, kv_local, GROUP, HD), jnp.float32),
    )
    prompt_pair = jnp.stack([prompt_keys, prompt_values])
    fragment = lax.all_gather(prompt_pair, "seq", axis=1, tiled=True)
    frag_rows = fragment.shape[1]
    key_block = fragment[0].reshape(frag_rows, kv_local, HD)
    value_block = fragment[1].reshape(frag_rows, kv_local, HD)
    softmax_state = update_state(softmax_state, grouped, key_block, value_block, None, scale_factor)
    response_pair = jnp.stack([response_keys, response_values])
    fragment = lax.all_gather(response_pair, "seq", axis=1, tiled=True)
    frag_rows = fragment.shape[1]
    key_pos = jnp.arange(frag_rows, dtype=jnp.int32)
    visible = (key_pos[None, :] <= positions[:, None]) & (key_pos[None, :] >= own_start[:, None])
    key_block = fragment[0].reshape(frag_rows, kv_local, HD)
    value_block = fragment[1].reshape(frag_rows, kv_local, HD)
    softmax_state = update_state(
        softmax_state, grouped, key_block, value_block, visible, scale_factor
    )
    maximum, summed, weighted = softmax_state
    attended = (
        (weighted / summed[..., None])
        .astype(jnp.bfloat16)
        .reshape(row_count, kv_local * GROUP * HD)
    )
    partial_out = jnp.dot(attended, out_weight, preferred_element_type=jnp.float32)
    return lax.psum_scatter(partial_out.astype(jnp.bfloat16), "tp", scatter_dimension=1, tiled=True)


def pack_kernel(meta, *refs, group):
    sources, targets, raw, sems = refs[:4], refs[4 : 4 + group], refs[4 + group], refs[5 + group]
    split = sources[0].shape[0]
    copies = []
    for d in range(group):
        at = pl.ds(pl.multiple_of((meta[0] ^ d) * HD, HD), HD)
        for n, source in enumerate(sources):
            side = pl.ds((n % 2) * HD, HD)
            rows = pl.ds(0 if n < 2 else split, source.shape[0])
            copies.append((source.at[:, at], targets[d].at[rows, side]))
            if n < 2:
                copies.append((source.at[:, at], raw.at[pl.ds(d * split, split), side]))
    started = [
        pltpu.make_async_copy(source, target, sems.at[n])
        for n, (source, target) in enumerate(copies)
    ]
    for copy in started:
        copy.start()
    for copy in started:
        copy.wait()


def pack_call(meta, arrays, group):
    split = arrays[0].shape[0]
    rows = split + arrays[2].shape[0]
    dtype = arrays[0].dtype
    return pl.pallas_call(
        functools.partial(pack_kernel, group=group),
        in_specs=[SMEM] + [pl.BlockSpec(memory_space=pltpu.HBM)] * 4,
        out_specs=[VMEM] * (group + 1),
        out_shape=[jax.ShapeDtypeStruct((rows, 2 * HD), dtype)] * group
        + [jax.ShapeDtypeStruct((split * group, 2 * HD), dtype)],
        scratch_shapes=[pltpu.SemaphoreType.DMA((6 * group,))],
        compiler_params=pltpu.CompilerParams(**PARAMS),
        cost_estimate=SMALL,
        name="pack",
    )(meta, *[pltpu.with_memory_space_constraint(a, pltpu.HBM) for a in arrays])


def regroup_kernel(*refs, group):
    sources, targets = refs[:-group], refs[-group:]
    rows = sources[0].shape[0] // group
    for d, target in enumerate(targets):
        for n, source in enumerate(sources):
            target[n * rows : (n + 1) * rows, :] = source[d * rows : (d + 1) * rows, :]


def regroup_call(arrays, group):
    rows, width = arrays[0].shape
    return pl.pallas_call(
        functools.partial(regroup_kernel, group=group),
        in_specs=[VMEM] * len(arrays),
        out_specs=[VMEM] * group,
        out_shape=[jax.ShapeDtypeStruct((rows // group * len(arrays), width), arrays[0].dtype)]
        * group,
        compiler_params=pltpu.CompilerParams(**PARAMS),
        cost_estimate=SMALL,
        name="regroup",
    )(*arrays)


def pick_kernel(meta, source, *refs, places):
    targets, sems = refs[:-1], refs[-1]
    started = []
    for n, d in enumerate(places):
        at = pl.ds(pl.multiple_of((meta[0] ^ d) * WIDE, WIDE), WIDE)
        started.append(pltpu.make_async_copy(source.at[:, at], targets[n], sems.at[n]))
    for copy in started:
        copy.start()
    for copy in started:
        copy.wait()


def pick_call(meta, array, places):
    return pl.pallas_call(
        functools.partial(pick_kernel, places=places),
        in_specs=[SMEM, pl.BlockSpec(memory_space=pltpu.HBM)],
        out_specs=[VMEM] * len(places),
        out_shape=[jax.ShapeDtypeStruct((array.shape[0], WIDE), array.dtype)] * len(places),
        scratch_shapes=[pltpu.SemaphoreType.DMA((len(places),))],
        compiler_params=pltpu.CompilerParams(**PARAMS),
        cost_estimate=SMALL,
        name="pick",
    )(meta, pltpu.with_memory_space_constraint(array, pltpu.HBM))


def join_kernel(*refs, bounds):
    count = len(refs) - len(bounds) + 1
    for n, (low, high) in enumerate(zip(bounds, bounds[1:])):
        for d in range(count):
            refs[count + n][d * (high - low) : (d + 1) * (high - low), :] = refs[d][low:high, :]


def join_call(parts, bounds):
    width, count = parts[0].shape[1], len(parts)
    return pl.pallas_call(
        functools.partial(join_kernel, bounds=bounds),
        in_specs=[VMEM] * count,
        out_specs=[VMEM] * (len(bounds) - 1),
        out_shape=[
            jax.ShapeDtypeStruct(((high - low) * count, width), parts[0].dtype)
            for low, high in zip(bounds, bounds[1:])
        ],
        compiler_params=pltpu.CompilerParams(**PARAMS),
        cost_estimate=SMALL,
        name="join",
    )(*parts)


def attend_kernel(
    meta, lengths, *refs, kinds, group, rows, offset, has_state, piece, quarter, scale
):
    refs = list(refs)
    q_ref = refs.pop(0)
    kv_refs = [refs.pop(0) for _ in kinds]
    if has_state:
        del refs[:2]
    if quarter is not None:
        weight = refs.pop(0)
    count = q_ref.shape[0] // rows
    final = piece is not None
    out_refs = [refs.pop(0) for _ in range(count if final else 0)]
    acc_ref, max_ref = refs.pop(0), refs.pop(0)
    heads = range(GROUP)
    pair = 2 * rows
    part = rows // PIECES if final else rows
    copies = []
    if quarter is not None:
        held, sems = refs
        width = held.shape[1]
        column = pl.multiple_of(meta[2 + quarter // 2] + (quarter % 2) * width, HD)
        for d in range(group):
            at = pl.ds(pl.multiple_of((meta[0] ^ d) * WIDE, WIDE), WIDE)
            copies.append(
                pltpu.make_async_copy(
                    weight.at[at, pl.ds(column, width)],
                    held.at[pl.ds(d * WIDE, WIDE), :],
                    sems.at[d],
                )
            )
    for copy in copies:
        copy.start()

    def across(x, width):
        return x if width == HD else jnp.concatenate([x] * (width // HD), axis=1)

    def first_of(position, zero):
        start, found = jnp.int32(0), zero
        for r in range(lengths.shape[0]):
            found = jnp.where(start <= position, start, found)
            start = start + lengths[r]
        return found

    def row_block(i, carry):
        skip = part * piece if final else 0
        here = pl.ds(pl.multiple_of(i * rows + skip, part), part)
        row_base = (meta[1] * group + (meta[0] ^ (offset + i))) * rows + skip

        def update(kv_ref, at, visible, fresh):
            keys = kv_ref[at, :HD]
            values = kv_ref[at, HD:]
            wide = jnp.concatenate([values, jnp.ones_like(values)], axis=1)
            if not fresh:
                old = [max_ref[h, here, :] for h in heads]
                kept = [acc_ref[h, here, :] for h in heads]
            tops, parts = [], []
            for h in heads:
                q = q_ref[here, h * HD : (h + 1) * HD]
                s = lax.dot_general(
                    q, keys, (((1,), (1,)), ((), ())), preferred_element_type=jnp.float32
                )
                if visible is not None:
                    s = jnp.where(visible, s, LOW)
                top = jnp.broadcast_to(jnp.max(s, axis=1, keepdims=True), (part, HD))
                if not fresh:
                    top = jnp.maximum(old[h], top)
                p = jnp.exp2((s - across(top, s.shape[1])) * scale).astype(jnp.bfloat16)
                term = jnp.dot(p, wide, preferred_element_type=jnp.float32)
                if not fresh:
                    term = kept[h] * across(jnp.exp2((old[h] - top) * scale), 2 * HD) + term
                tops.append(top)
                parts.append(term)
            for h in heads:
                acc_ref[h, here, :] = parts[h]
                max_ref[h, here, :] = tops[h]

        fresh = not has_state
        for kind, kv_ref in zip(kinds, kv_refs):
            if kind is None:
                step = min(kv_ref.shape[0], 512)
                for c in range(kv_ref.shape[0] // step):
                    update(kv_ref, slice(c * step, (c + 1) * step), None, fresh)
                    fresh = False
                continue
            first_low = first_of(row_base, jnp.int32(0))
            first_high = first_of(row_base + part - 1, jnp.int32(0))
            for j in range(group // 2):
                key_base = ((meta[1] - kind) * group + ((meta[0] ^ (2 * j)) & ~1)) * rows
                needed = (key_base <= row_base + part - 1) & (key_base + pair - 1 >= first_low)
                whole = (key_base + pair - 1 <= row_base) & (key_base >= first_high)
                at = slice(j * pair, (j + 1) * pair)

                @pl.when(needed & whole)
                def _(kv_ref=kv_ref, at=at):
                    update(kv_ref, at, None, False)

                @pl.when(needed & jnp.logical_not(whole))
                def _(kv_ref=kv_ref, at=at, key_base=key_base):
                    position = row_base + lax.broadcasted_iota(jnp.int32, (part, HD), 0)
                    first = first_of(position, jnp.zeros((part, HD), jnp.int32))
                    key_pos = key_base + (
                        lax.broadcasted_iota(jnp.int32, (part, pair), 1) ^ ((meta[0] & 1) * rows)
                    )
                    visible = (key_pos >= across(first, pair)) & (key_pos <= across(position, pair))
                    update(kv_ref, at, visible, False)

        for n, out_ref in enumerate(out_refs):

            @pl.when(i == n)
            def _(n=n, out_ref=out_ref):
                at = pl.ds(n * rows + part * piece, part)
                for h in heads:
                    out_ref[:, h * HD : (h + 1) * HD] = (
                        acc_ref[h, at, :HD] / acc_ref[h, at, HD:]
                    ).astype(jnp.bfloat16)

        return carry

    lax.fori_loop(0, count, row_block, 0)
    for copy in copies:
        copy.wait()


def attend_call(
    meta, lengths, q, pieces, state, group, rows, offset, piece=None, weight=None, quarter=None
):
    kinds = tuple(kind for kind, _ in pieces)
    arrays = [array for _, array in pieces]
    operands = [meta, lengths, q] + arrays + list(state or ())
    out_shape = [
        jax.ShapeDtypeStruct((GROUP, q.shape[0], 2 * HD), jnp.float32),
        jax.ShapeDtypeStruct((GROUP, q.shape[0], HD), jnp.float32),
    ]
    in_specs = [SMEM, SMEM] + [VMEM] * (len(operands) - 2)
    aliases, scratch, done = {}, [], 0
    if piece is not None:
        done = q.shape[0] // rows
        out_shape = [jax.ShapeDtypeStruct((rows // PIECES, WIDE), jnp.bfloat16)] * done + out_shape
    if state is not None:
        aliases = {len(operands) - 2: done, len(operands) - 1: done + 1}
    if quarter is not None:
        operands.append(pltpu.with_memory_space_constraint(weight, pltpu.HBM))
        in_specs.append(pl.BlockSpec(memory_space=pltpu.HBM))
        out_shape.append(
            jax.ShapeDtypeStruct((weight.shape[0], weight.shape[1] // 4), weight.dtype)
        )
        scratch = [pltpu.SemaphoreType.DMA((group,))]
    return pl.pallas_call(
        functools.partial(
            attend_kernel,
            kinds=kinds,
            group=group,
            rows=rows,
            offset=offset,
            has_state=state is not None,
            piece=piece,
            quarter=quarter,
            scale=HD**-0.5 * LOG2E,
        ),
        in_specs=in_specs,
        out_specs=[VMEM] * len(out_shape),
        out_shape=out_shape,
        scratch_shapes=scratch,
        input_output_aliases=aliases,
        compiler_params=pltpu.CompilerParams(**PARAMS),
        cost_estimate=LARGE,
        name="attend",
    )(*operands)


def project_kernel(*refs, spans, count):
    parts, weights, outs = refs[: count], refs[count : count + len(spans)], refs[count + len(spans) :]
    group = count // len(outs) if len(outs) == PIECES else count
    lines = []
    for n in range(0, count, group):
        lines.append(jnp.concatenate([part[...] for part in parts[n : n + group]], axis=1))
    rows = jnp.concatenate(lines, axis=0) if len(lines) > 1 else lines[0]
    size = lines[0].shape[0]
    low = 0
    for weight, (first, width) in zip(weights, spans):
        for at in range(0, width, TILE):
            wide = min(TILE, width - at)
            term = jnp.dot(
                rows, weight[:, first + at : first + at + wide], preferred_element_type=jnp.float32
            ).astype(jnp.bfloat16)
            for n, out in enumerate(outs):
                out[:, low + at : low + at + wide] = term[n * size : (n + 1) * size]
        low += width


def project_call(parts, weights, spans, outs):
    width = sum(span[1] for span in spans)
    size = parts[0].shape[0]
    return pl.pallas_call(
        functools.partial(project_kernel, spans=tuple(spans), count=len(parts)),
        in_specs=[VMEM] * (len(parts) + len(weights)),
        out_specs=[VMEM] * outs,
        out_shape=[jax.ShapeDtypeStruct((size, width), jnp.bfloat16)] * outs,
        compiler_params=pltpu.CompilerParams(**PARAMS),
        cost_estimate=SMALL,
        name="project",
    )(*parts, *weights)


def sum_kernel(*refs, widths):
    own, parts, out = refs[0], refs[1 : 1 + len(widths)], refs[-1]
    low = 0
    for part, width in zip(parts, widths):
        at = slice(low, low + width)
        out[:, at] = (own[:, at].astype(jnp.float32) + part[...].astype(jnp.float32)).astype(
            jnp.bfloat16
        )
        low += width


def sum_call(own, parts, piece, before):
    widths = tuple(part.shape[1] for part in parts)
    rows, width = own.shape
    rows *= PIECES
    here = pl.BlockSpec((rows // PIECES, width), lambda i: (piece, 0))
    operands = [own, *parts]
    in_specs = [pl.BlockSpec(own.shape, lambda i: (0, 0))] + [pl.BlockSpec(part.shape, lambda i: (0, 0)) for part in parts]
    aliases = {}
    if before is not None:
        aliases = {len(operands): 0}
        operands.append(before)
        in_specs.append(pl.BlockSpec(memory_space=pl.ANY))
    return pl.pallas_call(
        functools.partial(sum_kernel, widths=widths),
        grid=(1,),
        in_specs=in_specs,
        out_specs=here,
        out_shape=jax.ShapeDtypeStruct((rows, width), jnp.bfloat16),
        input_output_aliases=aliases,
        compiler_params=pltpu.CompilerParams(**PARAMS),
        cost_estimate=SMALL,
        name="sum",
    )(*operands)


def per_device_planes(
    queries,
    prompt_keys,
    prompt_values,
    response_keys,
    response_values,
    lengths,
    out_weight,
    *,
    n_seq,
    n_tp,
):
    rows = queries.shape[0]
    group = prompt_keys.shape[1] // HD
    levels = n_seq // group
    seq = lax.axis_index("seq")
    me = lax.rem(seq, group)
    level = lax.div(seq, group)
    tp = lax.axis_index("tp")
    half = out_weight.shape[1] // n_tp
    meta = jnp.stack([me, level, (1 - tp) * half, tp * half]).astype(jnp.int32)

    def swap(x, d):
        return lax.ppermute(
            x, "seq", [(i, i - i % group + ((i % group) ^ d)) for i in range(n_seq)]
        )

    def shift(x, k, around):
        pairs = [(i, i + k * group) for i in range(n_seq)]
        if around:
            pairs = [(i, j % n_seq) for i, j in pairs]
        return lax.ppermute(x, "seq", [(i, j) for i, j in pairs if 0 <= j < n_seq])

    p_rows = prompt_keys.shape[0]
    *sent, raw = pack_call(
        meta, [prompt_keys, prompt_values, response_keys, response_values], group
    )
    raws = [shift(raw, k, True) for k in range(1, levels)]
    got = [sent[0]] + [swap(sent[d], d) for d in range(1, group)]
    prompt, response = join_call(got, (0, p_rows, p_rows + rows))
    def attend(q, offset, pieces, state, piece=None, quarter=None):
        return attend_call(
            meta, lengths, q, pieces, state, group, rows, offset, piece, out_weight, quarter
        )

    def after(x, *earlier):
        return lax.optimization_barrier((x, *earlier))[0]

    picked = pick_call(meta, after(queries, sent[0]), tuple(range(group)))
    (q_near,) = join_call([picked[0], swap(picked[1], 1)], (0, rows))
    distant = [swap(after(picked[d], response), d) for d in (2, 3)]
    (q_far,) = join_call(distant, (0, rows))

    own_keys = [(None, prompt), (0, response)]
    *near, held0 = attend(q_near, 0, own_keys, None, quarter=0)
    regrouped = regroup_call([after(x, near[1]) for x in raws], group)
    (others,) = join_call(
        [regrouped[0]] + [swap(regrouped[d], d) for d in range(1, group)],
        (0, regrouped[0].shape[0]),
    )
    back1 = shift(after(response, regrouped[0]), 1, False)
    *far, held1 = attend(after(q_far, regrouped[0]), 2, own_keys, None, quarter=1)
    back1 = after(back1, far[1])
    back2 = shift(back1, 1, False)
    *far, held2 = attend(q_far, 2, [(1, back1), (None, others)], far, quarter=2)
    *near, held3 = attend(
        after(q_near, far[1]), 0, [(1, back1), (None, others)], near, quarter=3
    )
    back2 = after(back2, near[1])
    parts = []
    for c in range(PIECES):
        block2, block3, *far = attend(q_far, 2, [(2, back2)], far, piece=c)
        block0, block1, *near = attend(q_near, 0, [(2, back2)], near, piece=c)
        parts.append([block0, swap(block1, 1), swap(block2, 2), swap(block3, 3)])

    quarter = half // 2
    small = quarter // 5 * 2
    spans = [(held0, 0, small), (held0, small, quarter - small), (held1, 0, quarter)]
    came = []
    for c in range(PIECES):
        came.append([])
        for held, first, width in spans:
            (term,) = project_call(parts[c], [held], [(first, width)], 1)
            came[c].append(lax.ppermute(term, "tp", [(0, 1), (1, 0)]))
    own = project_call(
        parts[0] + parts[1], [held2, held3], [(0, quarter), (0, quarter)], PIECES
    )
    out = None
    for c in range(PIECES):
        out = sum_call(own[c], came[c], c, out)
    return out


def solution(mesh):
    in_specs = (
        P("seq", "tp"),
        P("seq", "tp"),
        P("seq", "tp"),
        P("seq", "tp"),
        P("seq", "tp"),
        P(),
        P("tp", None),
    )
    out_specs = P("seq", "tp")
    n_seq, n_tp = mesh.shape["seq"], mesh.shape["tp"]
    if n_tp == 2 and n_seq == 16:
        body = functools.partial(per_device_planes, n_seq=n_seq, n_tp=n_tp)
    else:
        body = per_device_general
    return jax.shard_map(body, mesh=mesh, in_specs=in_specs, out_specs=out_specs, check_vma=False)
```

```python
import functools

import jax
import jax.numpy as jnp
from jax import lax
from jax.experimental import pallas as pl
from jax.experimental.pallas import tpu as pltpu
from jax.sharding import PartitionSpec as P

HEADS = 40
KVH = 8
HD = 128
GROUP = HEADS // KVH
WIDE = GROUP * HD
LOG2E = 1.4426950408889634
LOW = -1e30
PIECES = 2
SHARES = (3, 2, 3, 2)
TILE = 256
ANY = pl.BlockSpec(memory_space=pl.ANY)
VMEM = pl.BlockSpec(memory_space=pltpu.VMEM)
SMEM = pl.BlockSpec(memory_space=pltpu.SMEM)
SMALL = pl.CostEstimate(flops=1000, bytes_accessed=1000, transcendentals=0)
LARGE = pl.CostEstimate(flops=2 * 10**10, bytes_accessed=1000, transcendentals=0)
FIRST = pl.CostEstimate(flops=2 * 10**10, bytes_accessed=1000, transcendentals=0)
PARAMS = dict(vmem_limit_bytes=16 * 2**20)


def segment_layout(lengths, first_row, row_count):
    positions = first_row + jnp.arange(row_count, dtype=jnp.int32)
    seg_ends = jnp.cumsum(lengths)
    seg_starts = seg_ends - lengths
    inside = (positions[:, None] >= seg_starts[None, :]) & (positions[:, None] < seg_ends[None, :])
    own_start = jnp.sum(jnp.where(inside, seg_starts[None, :], 0), axis=1)
    return (positions, own_start)


def update_state(running, grouped, key_block, value_block, visible, scale_factor):
    maximum, summed, weighted = running
    scores = (
        jnp.einsum("rkgd,nkd->rkgn", grouped, key_block, preferred_element_type=jnp.float32)
        * scale_factor
    )
    if visible is not None:
        scores = jnp.where(visible[:, None, None, :], scores, -jnp.inf)
    new_max = jnp.maximum(maximum, jnp.max(scores, axis=3))
    weights = jnp.exp(scores - new_max[..., None])
    rescale = jnp.exp(maximum - new_max)
    rounded = weights.astype(jnp.bfloat16)
    summed = summed * rescale + jnp.sum(weights, axis=3)
    weighted = weighted * rescale[..., None] + jnp.einsum(
        "rkgn,nkd->rkgd", rounded, value_block, preferred_element_type=jnp.float32
    )
    return (new_max, summed, weighted)


def per_device_general(
    queries, prompt_keys, prompt_values, response_keys, response_values, lengths, out_weight
):
    row_count = queries.shape[0]
    kv_local = prompt_keys.shape[1] // HD
    scale_factor = HD ** (-0.5)
    grouped = queries.reshape(row_count, kv_local, GROUP, HD)
    first_row = lax.axis_index("seq") * row_count
    positions, own_start = segment_layout(lengths, first_row, row_count)
    softmax_state = (
        jnp.full((row_count, kv_local, GROUP), -jnp.inf, jnp.float32),
        jnp.zeros((row_count, kv_local, GROUP), jnp.float32),
        jnp.zeros((row_count, kv_local, GROUP, HD), jnp.float32),
    )
    prompt_pair = jnp.stack([prompt_keys, prompt_values])
    fragment = lax.all_gather(prompt_pair, "seq", axis=1, tiled=True)
    frag_rows = fragment.shape[1]
    key_block = fragment[0].reshape(frag_rows, kv_local, HD)
    value_block = fragment[1].reshape(frag_rows, kv_local, HD)
    softmax_state = update_state(softmax_state, grouped, key_block, value_block, None, scale_factor)
    response_pair = jnp.stack([response_keys, response_values])
    fragment = lax.all_gather(response_pair, "seq", axis=1, tiled=True)
    frag_rows = fragment.shape[1]
    key_pos = jnp.arange(frag_rows, dtype=jnp.int32)
    visible = (key_pos[None, :] <= positions[:, None]) & (key_pos[None, :] >= own_start[:, None])
    key_block = fragment[0].reshape(frag_rows, kv_local, HD)
    value_block = fragment[1].reshape(frag_rows, kv_local, HD)
    softmax_state = update_state(
        softmax_state, grouped, key_block, value_block, visible, scale_factor
    )
    maximum, summed, weighted = softmax_state
    attended = (
        (weighted / summed[..., None])
        .astype(jnp.bfloat16)
        .reshape(row_count, kv_local * GROUP * HD)
    )
    partial_out = jnp.dot(attended, out_weight, preferred_element_type=jnp.float32)
    return lax.psum_scatter(partial_out.astype(jnp.bfloat16), "tp", scatter_dimension=1, tiled=True)


def pack_kernel(meta, *refs, group):
    sources, (kept, given, raw, sems) = refs[:4], refs[4:]
    split = sources[0].shape[0]
    size = split + sources[2].shape[0]
    copies = []
    for d in range(group):
        at = pl.ds(pl.multiple_of((meta[0] ^ d) * HD, HD), HD)
        target = given if d % 2 else kept
        for n, source in enumerate(sources):
            side = pl.ds((n % 2) * HD, HD)
            rows = pl.ds(d // 2 * size + (0 if n < 2 else split), source.shape[0])
            copies.append((source.at[:, at], target.at[rows, side]))
            if n < 2:
                copies.append((source.at[:, at], raw.at[pl.ds(d * split, split), side]))
    run_copies(copies, sems)


def run_copies(copies, sems):
    started = [
        pltpu.make_async_copy(source, target, sems.at[n])
        for n, (source, target) in enumerate(copies)
    ]
    for copy in started:
        copy.start()
    for copy in started:
        copy.wait()


def pack_call(meta, arrays, group):
    split = arrays[0].shape[0]
    rows = split + arrays[2].shape[0]
    dtype = arrays[0].dtype
    return pl.pallas_call(
        functools.partial(pack_kernel, group=group),
        in_specs=[SMEM] + [pl.BlockSpec(memory_space=pltpu.HBM)] * 4,
        out_specs=[VMEM] * 3,
        out_shape=[jax.ShapeDtypeStruct((group // 2 * rows, 2 * HD), dtype)] * 2
        + [jax.ShapeDtypeStruct((split * group, 2 * HD), dtype)],
        scratch_shapes=[pltpu.SemaphoreType.DMA((6 * group,))],
        compiler_params=pltpu.CompilerParams(**PARAMS),
        cost_estimate=SMALL,
        name="pack",
    )(meta, *[pltpu.with_memory_space_constraint(a, pltpu.HBM) for a in arrays])


def regroup_kernel(*refs):
    sources, targets = refs[:-3], refs[-2:]
    rows = sources[0].shape[0] // 4
    size = rows * len(sources)
    for d in range(4):
        for n, source in enumerate(sources):
            low = d // 2 * size + n * rows
            targets[d % 2][low : low + rows, :] = source[d * rows : (d + 1) * rows, :]


def regroup_call(arrays, wait):
    rows, width = arrays[0].shape
    return pl.pallas_call(
        regroup_kernel,
        in_specs=[VMEM] * len(arrays) + [ANY],
        out_specs=[VMEM] * 2,
        out_shape=[jax.ShapeDtypeStruct((rows // 2 * len(arrays), width), arrays[0].dtype)] * 2,
        compiler_params=pltpu.CompilerParams(**PARAMS),
        cost_estimate=SMALL,
        name="regroup",
    )(*arrays, wait)


def pick_kernel(meta, source, wait, kept, given, sems):
    rows = source.shape[0]
    copies = []
    for d in range(4):
        at = pl.ds(pl.multiple_of((meta[0] ^ d) * WIDE, WIDE), WIDE)
        target = given if d % 2 else kept
        copies.append((source.at[:, at], target.at[pl.ds(d // 2 * rows, rows), :]))
    run_copies(copies, sems)


def pick_call(meta, array, wait):
    rows = array.shape[0]
    return pl.pallas_call(
        pick_kernel,
        in_specs=[SMEM, pl.BlockSpec(memory_space=pltpu.HBM), ANY],
        out_specs=[VMEM] * 2,
        out_shape=[jax.ShapeDtypeStruct((2 * rows, WIDE), array.dtype)] * 2,
        scratch_shapes=[pltpu.SemaphoreType.DMA((4,))],
        compiler_params=pltpu.CompilerParams(**PARAMS),
        cost_estimate=SMALL,
        name="pick",
    )(meta, pltpu.with_memory_space_constraint(array, pltpu.HBM), wait)


def turn_kernel(kept, came, *refs, pieces):
    near, onward = refs[-2:]
    size = kept.shape[0] // 2
    part = size // pieces
    for c in range(pieces):
        for n, source in enumerate((kept, came)):
            at = (2 * c + n) * part
            near[at : at + part, :] = source[c * part : (c + 1) * part, :]
            onward[at : at + part, :] = source[size + c * part : size + (c + 1) * part, :]


def turn_call(kept, came, *wait, pieces=1):
    return pl.pallas_call(
        functools.partial(turn_kernel, pieces=pieces),
        in_specs=[VMEM] * 2 + [ANY] * len(wait),
        out_specs=[VMEM] * 2,
        out_shape=[jax.ShapeDtypeStruct(kept.shape, kept.dtype)] * 2,
        compiler_params=pltpu.CompilerParams(**PARAMS),
        cost_estimate=SMALL,
        name="turn",
    )(kept, came, *wait)


def join_kernel(*refs, groups, count, waits):
    for n, spans in enumerate(groups):
        at = 0
        for source in refs[:count]:
            for low, high in spans:
                refs[count + waits + n][at : at + high - low, :] = source[low:high, :]
                at += high - low


def join_call(parts, *groups, wait=()):
    width, count = parts[0].shape[1], len(parts)
    return pl.pallas_call(
        functools.partial(join_kernel, groups=groups, count=count, waits=len(wait)),
        in_specs=[VMEM] * count + [ANY] * len(wait),
        out_specs=[VMEM] * len(groups),
        out_shape=[
            jax.ShapeDtypeStruct(
                (count * sum(high - low for low, high in spans), width), parts[0].dtype
            )
            for spans in groups
        ],
        compiler_params=pltpu.CompilerParams(**PARAMS),
        cost_estimate=SMALL,
        name="join",
    )(*parts, *wait)


def share_of(half, n):
    unit = half // sum(SHARES)
    return sum(SHARES[:n]) * unit, SHARES[n] * unit


def weight_copies(meta, weight, targets, sems, fetch):
    copies = []
    half = weight.shape[1] // 2
    for n, (share, target) in enumerate(zip(fetch, targets)):
        start, width = share_of(half, share % len(SHARES))
        column = pl.multiple_of(meta[2 + share // len(SHARES)] + start, HD)
        for d in range(weight.shape[0] // WIDE):
            at = pl.ds(pl.multiple_of((meta[0] ^ d) * WIDE, WIDE), WIDE)
            copies.append(
                pltpu.make_async_copy(
                    weight.at[at, pl.ds(column, width)],
                    target.at[pl.ds(d * WIDE, WIDE), :],
                    sems.at[n, d],
                )
            )
    return copies


def attend_kernel(
    meta, lengths, *refs, kinds, group, rows, offset, has_state, piece, final, fetch, waits, scale
):
    refs = list(refs)
    q_ref = refs.pop(0)
    kv_refs = [refs.pop(0) for _ in kinds]
    if has_state:
        del refs[:2]
    if fetch:
        weight = refs.pop(0)
    del refs[:waits]
    out_refs = [refs.pop(0) for _ in range(final)]
    acc_ref, max_ref = refs.pop(0), refs.pop(0)
    heads = range(GROUP)
    pair = 2 * rows
    part = rows // PIECES
    copies = []
    if fetch:
        copies = weight_copies(meta, weight, refs[:-1], refs[-1], fetch)
    for copy in copies:
        copy.start()

    def across(x, width):
        return x if width == HD else jnp.concatenate([x] * (width // HD), axis=1)

    def first_of(position, zero):
        start, found = jnp.int32(0), zero
        for r in range(lengths.shape[0]):
            found = jnp.where(start <= position, start, found)
            start = start + lengths[r]
        return found

    def row_block(i, carry):
        here = pl.ds(pl.multiple_of(i * rows, rows), rows)
        bases = [
            (meta[1] * group + (meta[0] ^ (offset + n))) * rows + i * part for n in range(PIECES)
        ]
        lowest = jnp.minimum(*bases)
        highest = jnp.maximum(*bases) + part - 1

        def update(kv_ref, at, visible, fresh):
            keys = kv_ref[at, :HD]
            values = kv_ref[at, HD:]
            wide = jnp.concatenate([values, jnp.ones_like(values)], axis=1)
            if not fresh:
                old = [max_ref[h, here, :] for h in heads]
                kept = [acc_ref[h, here, :] for h in heads]
            tops, parts = [], []
            for h in heads:
                q = q_ref[here, h * HD : (h + 1) * HD]
                s = lax.dot_general(
                    q, keys, (((1,), (1,)), ((), ())), preferred_element_type=jnp.float32
                )
                if visible is not None:
                    s = jnp.where(visible, s, LOW)
                top = jnp.broadcast_to(jnp.max(s, axis=1, keepdims=True), (rows, HD))
                if not fresh:
                    top = jnp.maximum(old[h], top)
                p = jnp.exp2((s - across(top, s.shape[1])) * scale).astype(jnp.bfloat16)
                term = jnp.dot(p, wide, preferred_element_type=jnp.float32)
                if not fresh:
                    term = kept[h] * across(jnp.exp2((old[h] - top) * scale), 2 * HD) + term
                tops.append(top)
                parts.append(term)
            for h in heads:
                acc_ref[h, here, :] = parts[h]
                max_ref[h, here, :] = tops[h]

        fresh = not has_state
        for kind, kv_ref in zip(kinds, kv_refs):
            if kind is None:
                for low in range(0, kv_ref.shape[0], 512):
                    update(kv_ref, slice(low, min(low + 512, kv_ref.shape[0])), None, fresh)
                    fresh = False
                continue
            first_low = first_of(lowest, jnp.int32(0))
            first_high = first_of(highest, jnp.int32(0))
            for j in range(group // 2):
                key_base = ((meta[1] - kind) * group + ((meta[0] ^ (2 * j)) & ~1)) * rows
                needed = (key_base <= highest) & (key_base + pair - 1 >= first_low)
                whole = (key_base + pair - 1 <= lowest) & (key_base >= first_high)
                at = slice(j * pair, (j + 1) * pair)

                @pl.when(needed & whole)
                def _(kv_ref=kv_ref, at=at):
                    update(kv_ref, at, None, False)

                @pl.when(needed & jnp.logical_not(whole))
                def _(kv_ref=kv_ref, at=at, key_base=key_base):
                    line = lax.broadcasted_iota(jnp.int32, (rows, HD), 0)
                    position = line + jnp.where(line < part, bases[0], bases[1] - part)
                    first = first_of(position, jnp.zeros((rows, HD), jnp.int32))
                    key_pos = key_base + (
                        lax.broadcasted_iota(jnp.int32, (rows, pair), 1) ^ ((meta[0] & 1) * rows)
                    )
                    visible = (key_pos >= across(first, pair)) & (key_pos <= across(position, pair))
                    update(kv_ref, at, visible, False)

        for out_ref in out_refs:
            for h in heads:
                out_ref[:, h * HD : (h + 1) * HD] = (
                    acc_ref[h, here, :HD] / acc_ref[h, here, HD:]
                ).astype(jnp.bfloat16)
        return carry

    if piece is None:
        lax.fori_loop(0, q_ref.shape[0] // rows, row_block, 0)
    else:
        row_block(piece, 0)
    for copy in copies:
        copy.wait()


def attend_call(
    meta, lengths, q, pieces, state, group, rows, offset, piece=None, final=False, weight=None, fetch=(), cost=None, wait=()
):
    kinds = tuple(kind for kind, _ in pieces)
    arrays = [array for _, array in pieces]
    operands = [meta, lengths, q] + arrays + list(state or ())
    out_shape = [
        jax.ShapeDtypeStruct((GROUP, q.shape[0], 2 * HD), jnp.float32),
        jax.ShapeDtypeStruct((GROUP, q.shape[0], HD), jnp.float32),
    ]
    in_specs = [SMEM, SMEM] + [VMEM] * (len(operands) - 2)
    aliases, scratch, done = {}, [], 0
    if final:
        done = 1
        out_shape = [jax.ShapeDtypeStruct((rows, WIDE), jnp.bfloat16)] + out_shape
    if state is not None:
        aliases = {len(operands) - 2: done, len(operands) - 1: done + 1}
    if fetch:
        operands.append(pltpu.with_memory_space_constraint(weight, pltpu.HBM))
        in_specs.append(pl.BlockSpec(memory_space=pltpu.HBM))
        for share in fetch:
            width = share_of(weight.shape[1] // 2, share % len(SHARES))[1]
            out_shape.append(jax.ShapeDtypeStruct((weight.shape[0], width), weight.dtype))
        scratch = [pltpu.SemaphoreType.DMA((len(fetch), group))]
    operands += wait
    in_specs += [ANY] * len(wait)
    return pl.pallas_call(
        functools.partial(
            attend_kernel,
            kinds=kinds,
            group=group,
            rows=rows,
            offset=offset,
            has_state=state is not None,
            piece=piece,
            final=final,
            fetch=fetch,
            waits=len(wait),
            scale=HD**-0.5 * LOG2E,
        ),
        in_specs=in_specs,
        out_specs=[VMEM] * len(out_shape),
        out_shape=out_shape,
        scratch_shapes=scratch,
        input_output_aliases=aliases,
        compiler_params=pltpu.CompilerParams(**PARAMS),
        cost_estimate=cost or LARGE,
        name="attend",
    )(*operands)


def project_kernel(*refs, spans, count, waits, fetch):
    refs = list(refs)
    parts = [refs.pop(0) for _ in range(count)]
    weights = [refs.pop(0) for _ in range(len(spans) - len(fetch))]
    copies = []
    if fetch:
        *targets, sems = refs[-1 - len(fetch) :]
        copies = weight_copies(refs[0], refs[1], targets, sems, fetch)
        weights += targets
        refs = refs[2 : -1 - len(fetch)]
    outs = refs[waits:]
    for copy in copies:
        copy.start()
    lines = []
    for n in range(0, count, 3):
        near, other, far = parts[n : n + 3]
        size = near.shape[0] // 2
        lines.append(
            jnp.concatenate([near[:size], other[:size], far[:size], other[size:]], axis=1)
        )
    rows = jnp.concatenate(lines, axis=0) if len(lines) > 1 else lines[0]
    low = 0
    for k, (weight, (first, width)) in enumerate(zip(weights, spans)):
        n = k - (len(spans) - len(fetch))
        if n >= 0:
            each = len(copies) // len(fetch)
            for copy in copies[n * each : (n + 1) * each]:
                copy.wait()
        for at in range(0, width, TILE):
            wide = min(TILE, width - at)
            term = jnp.dot(
                rows, weight[:, first + at : first + at + wide], preferred_element_type=jnp.float32
            ).astype(jnp.bfloat16)
            for n, out in enumerate(outs):
                out[:, low + at : low + at + wide] = term[n * size : (n + 1) * size]
        low += width


def project_call(parts, weights, spans, outs, wait=(), meta=None, weight=None, fetch=()):
    width = sum(span[1] for span in spans)
    size = parts[0].shape[0] // 2
    operands = [*parts, *weights]
    in_specs = [VMEM] * len(operands)
    scratch = []
    if fetch:
        operands += [meta, pltpu.with_memory_space_constraint(weight, pltpu.HBM)]
        in_specs += [SMEM, pl.BlockSpec(memory_space=pltpu.HBM)]
        scratch = [
            pltpu.VMEM((weight.shape[0], wide), weight.dtype) for _, wide in spans[-len(fetch) :]
        ] + [pltpu.SemaphoreType.DMA((len(fetch), weight.shape[0] // WIDE))]
    return pl.pallas_call(
        functools.partial(
            project_kernel, spans=tuple(spans), count=len(parts), waits=len(wait), fetch=fetch
        ),
        in_specs=in_specs + [ANY] * len(wait),
        out_specs=[VMEM] * outs,
        out_shape=[jax.ShapeDtypeStruct((size, width), jnp.bfloat16)] * outs,
        scratch_shapes=scratch,
        compiler_params=pltpu.CompilerParams(**PARAMS),
        cost_estimate=SMALL,
        name="project",
    )(*operands, *wait)


def sum_kernel(*refs, widths):
    own, parts, out = refs[0], refs[1 : 1 + len(widths)], refs[-1]
    low = 0
    for part, width in zip(parts, widths):
        at = slice(low, low + width)
        out[:, at] = (own[:, at].astype(jnp.float32) + part[...].astype(jnp.float32)).astype(
            jnp.bfloat16
        )
        low += width


def sum_call(own, parts, piece, before):
    widths = tuple(part.shape[1] for part in parts)
    rows, width = own.shape
    rows *= PIECES
    here = pl.BlockSpec((rows // PIECES, width), lambda i: (piece, 0))
    operands = [own, *parts]
    in_specs = [pl.BlockSpec(own.shape, lambda i: (0, 0))] + [pl.BlockSpec(part.shape, lambda i: (0, 0)) for part in parts]
    aliases = {}
    if before is not None:
        aliases = {len(operands): 0}
        operands.append(before)
        in_specs.append(pl.BlockSpec(memory_space=pl.ANY))
    return pl.pallas_call(
        functools.partial(sum_kernel, widths=widths),
        grid=(1,),
        in_specs=in_specs,
        out_specs=here,
        out_shape=jax.ShapeDtypeStruct((rows, width), jnp.bfloat16),
        input_output_aliases=aliases,
        compiler_params=pltpu.CompilerParams(**PARAMS),
        cost_estimate=SMALL,
        name="sum",
    )(*operands)


def per_device_planes(
    queries,
    prompt_keys,
    prompt_values,
    response_keys,
    response_values,
    lengths,
    out_weight,
    *,
    n_seq,
    n_tp,
):
    rows = queries.shape[0]
    group = prompt_keys.shape[1] // HD
    levels = n_seq // group
    seq = lax.axis_index("seq")
    me = lax.rem(seq, group)
    level = lax.div(seq, group)
    tp = lax.axis_index("tp")
    half = out_weight.shape[1] // n_tp
    meta = jnp.stack([me, level, (1 - tp) * half, tp * half]).astype(jnp.int32)

    def swap(x, d):
        return lax.ppermute(
            x, "seq", [(i, i - i % group + ((i % group) ^ d)) for i in range(n_seq)]
        )

    def shift(x, k, around):
        pairs = [(i, i + k * group) for i in range(n_seq)]
        if around:
            pairs = [(i, j % n_seq) for i, j in pairs]
        return lax.ppermute(x, "seq", [(i, j) for i, j in pairs if 0 <= j < n_seq])

    p_rows = prompt_keys.shape[0]
    kept, given, raw = pack_call(
        meta, [prompt_keys, prompt_values, response_keys, response_values], group
    )
    raws = [shift(raw, k, True) for k in range(1, levels)]
    close, onward = turn_call(kept, swap(given, 1))
    far_off = swap(onward, 2)
    size = p_rows + rows
    prompt, response = join_call(
        [close, far_off], ((0, p_rows), (size, size + p_rows)), ((p_rows, size), (size + p_rows, 2 * size))
    )

    def attend(q, offset, pieces, state, piece=None, final=False, fetch=(), cost=LARGE, wait=()):
        return attend_call(
            meta,
            lengths,
            q,
            pieces,
            state,
            group,
            rows,
            offset,
            piece,
            final,
            out_weight,
            fetch,
            cost,
            wait,
        )

    kept, given = pick_call(meta, queries, kept)
    q_near, onward = turn_call(kept, swap(given, 1), response, pieces=PIECES)
    q_far = swap(onward, 2)

    own_keys = [(None, prompt), (0, response)]
    back1 = shift(response, 1, False)
    near0, near1, *held = attend(q_near, 0, own_keys, None, fetch=(0, 1))
    near = [near0, near1]
    *far, share = attend(q_far, 2, own_keys, None, cost=SMALL, fetch=(2,), wait=near[1:])
    held.append(share)
    kept, given = regroup_call(raws, far[1])
    others0, onward = turn_call(kept, swap(given, 1))
    others1 = swap(onward, 2)
    back2 = shift(back1, 1, False)
    early, late = [(1, back1), (None, others0)], [(None, others1), (2, back2)]

    def project(part, low, high, wait=()):
        used = []
        for n in range(len(SHARES)):
            start, width = share_of(half, n)
            span = max(low - start, 0), min(high - start, width)
            if span[0] < span[1]:
                used.append((held[n], (span[0], span[1] - span[0])))
        (term,) = project_call(part, [a for a, _ in used], [b for _, b in used], 1, wait)
        return term

    def cross(term):
        return lax.ppermute(term, "tp", [(0, 1), (1, 0)])

    def bring(near_done, far_done, *wait):
        came = swap(far_done, 2)
        (give,) = join_call([near_done, came], ((rows // PIECES, rows),), wait=wait)
        return [near_done, swap(give, 1), came]

    *near, share = attend(q_near, 0, early, near, piece=0, fetch=(3,))
    held.append(share)
    *far, share = attend(q_far, 2, early, far, piece=0, fetch=(4,), cost=SMALL, wait=near[1:])
    held.append(share)
    far_done, *far = attend(q_far, 2, late, far, piece=0, final=True, cost=SMALL)
    near_done, *near = attend(q_near, 0, late, near, piece=0, final=True, wait=[far_done])
    far = attend(q_far, 2, early, far, piece=1, cost=SMALL, wait=[near_done])
    part0 = bring(near_done, far_done, far[1])
    terms = [project(part0, 0, half, far[1:])]
    came0 = [cross(term) for term in terms]

    far_done, *far = attend(q_far, 2, late, far, piece=1, final=True, wait=terms)
    near_done, *near, share = attend(
        q_near, 0, early + late, near, piece=1, final=True, fetch=(5,), wait=[far_done]
    )
    held.append(share)
    part1 = bring(near_done, far_done, near[1])
    terms = [project(part1, 0, half // 2)]
    terms.append(project(part1, half // 2, half, [came0[0], terms[0]]))
    came1 = [cross(term) for term in terms]
    came = [came0, came1]
    own = project_call(
        part0 + part1,
        held[len(SHARES) :],
        [(0, share_of(half, n)[1]) for n in range(len(SHARES))],
        PIECES,
        terms[1:],
        meta,
        out_weight,
        (6, 7),
    )
    out = None
    for c in range(PIECES):
        out = sum_call(own[c], came[c], c, out)
    return out


def solution(mesh):
    in_specs = (
        P("seq", "tp"),
        P("seq", "tp"),
        P("seq", "tp"),
        P("seq", "tp"),
        P("seq", "tp"),
        P(),
        P("tp", None),
    )
    out_specs = P("seq", "tp")
    n_seq, n_tp = mesh.shape["seq"], mesh.shape["tp"]
    if n_tp == 2 and n_seq == 16:
        body = functools.partial(per_device_planes, n_seq=n_seq, n_tp=n_tp)
    else:
        body = per_device_general
    return jax.shard_map(body, mesh=mesh, in_specs=in_specs, out_specs=out_specs, check_vma=False)
```

```python
import functools

import jax
import jax.numpy as jnp
from jax import lax
from jax.experimental import pallas as pl
from jax.experimental.pallas import tpu as pltpu
from jax.sharding import PartitionSpec as P

HEADS = 40
KVH = 8
HD = 128
GROUP = HEADS // KVH
WIDE = GROUP * HD
LOG2E = 1.4426950408889634
LOW = -1e30
PIECES = (5, 3)
SHARES = (3, 2, 3, 2)
TILE = 256
ANY = pl.BlockSpec(memory_space=pl.ANY)
VMEM = pl.BlockSpec(memory_space=pltpu.VMEM)
SMEM = pl.BlockSpec(memory_space=pltpu.SMEM)
SMALL = pl.CostEstimate(flops=1000, bytes_accessed=1000, transcendentals=0)
LARGE = pl.CostEstimate(flops=2 * 10**10, bytes_accessed=1000, transcendentals=0)
FIRST = pl.CostEstimate(flops=2 * 10**10, bytes_accessed=1000, transcendentals=0)
PARAMS = dict(vmem_limit_bytes=16 * 2**20)


def segment_layout(lengths, first_row, row_count):
    positions = first_row + jnp.arange(row_count, dtype=jnp.int32)
    seg_ends = jnp.cumsum(lengths)
    seg_starts = seg_ends - lengths
    inside = (positions[:, None] >= seg_starts[None, :]) & (positions[:, None] < seg_ends[None, :])
    own_start = jnp.sum(jnp.where(inside, seg_starts[None, :], 0), axis=1)
    return (positions, own_start)


def update_state(running, grouped, key_block, value_block, visible, scale_factor):
    maximum, summed, weighted = running
    scores = (
        jnp.einsum("rkgd,nkd->rkgn", grouped, key_block, preferred_element_type=jnp.float32)
        * scale_factor
    )
    if visible is not None:
        scores = jnp.where(visible[:, None, None, :], scores, -jnp.inf)
    new_max = jnp.maximum(maximum, jnp.max(scores, axis=3))
    weights = jnp.exp(scores - new_max[..., None])
    rescale = jnp.exp(maximum - new_max)
    rounded = weights.astype(jnp.bfloat16)
    summed = summed * rescale + jnp.sum(weights, axis=3)
    weighted = weighted * rescale[..., None] + jnp.einsum(
        "rkgn,nkd->rkgd", rounded, value_block, preferred_element_type=jnp.float32
    )
    return (new_max, summed, weighted)


def per_device_general(
    queries, prompt_keys, prompt_values, response_keys, response_values, lengths, out_weight
):
    row_count = queries.shape[0]
    kv_local = prompt_keys.shape[1] // HD
    scale_factor = HD ** (-0.5)
    grouped = queries.reshape(row_count, kv_local, GROUP, HD)
    first_row = lax.axis_index("seq") * row_count
    positions, own_start = segment_layout(lengths, first_row, row_count)
    softmax_state = (
        jnp.full((row_count, kv_local, GROUP), -jnp.inf, jnp.float32),
        jnp.zeros((row_count, kv_local, GROUP), jnp.float32),
        jnp.zeros((row_count, kv_local, GROUP, HD), jnp.float32),
    )
    prompt_pair = jnp.stack([prompt_keys, prompt_values])
    fragment = lax.all_gather(prompt_pair, "seq", axis=1, tiled=True)
    frag_rows = fragment.shape[1]
    key_block = fragment[0].reshape(frag_rows, kv_local, HD)
    value_block = fragment[1].reshape(frag_rows, kv_local, HD)
    softmax_state = update_state(softmax_state, grouped, key_block, value_block, None, scale_factor)
    response_pair = jnp.stack([response_keys, response_values])
    fragment = lax.all_gather(response_pair, "seq", axis=1, tiled=True)
    frag_rows = fragment.shape[1]
    key_pos = jnp.arange(frag_rows, dtype=jnp.int32)
    visible = (key_pos[None, :] <= positions[:, None]) & (key_pos[None, :] >= own_start[:, None])
    key_block = fragment[0].reshape(frag_rows, kv_local, HD)
    value_block = fragment[1].reshape(frag_rows, kv_local, HD)
    softmax_state = update_state(
        softmax_state, grouped, key_block, value_block, visible, scale_factor
    )
    maximum, summed, weighted = softmax_state
    attended = (
        (weighted / summed[..., None])
        .astype(jnp.bfloat16)
        .reshape(row_count, kv_local * GROUP * HD)
    )
    partial_out = jnp.dot(attended, out_weight, preferred_element_type=jnp.float32)
    return lax.psum_scatter(partial_out.astype(jnp.bfloat16), "tp", scatter_dimension=1, tiled=True)


def pack_kernel(meta, *refs, group):
    sources, (kept, given, raw, sems) = refs[:4], refs[4:]
    split = sources[0].shape[0]
    size = split + sources[2].shape[0]
    copies = []
    for d in range(group):
        at = pl.ds(pl.multiple_of((meta[0] ^ d) * HD, HD), HD)
        target = given if d % 2 else kept
        for n, source in enumerate(sources):
            side = pl.ds((n % 2) * HD, HD)
            rows = pl.ds(d // 2 * size + (0 if n < 2 else split), source.shape[0])
            copies.append((source.at[:, at], target.at[rows, side]))
            if n < 2:
                copies.append((source.at[:, at], raw.at[pl.ds(d * split, split), side]))
    run_copies(copies, sems)


def run_copies(copies, sems):
    started = [
        pltpu.make_async_copy(source, target, sems.at[n])
        for n, (source, target) in enumerate(copies)
    ]
    for copy in started:
        copy.start()
    for copy in started:
        copy.wait()


def pack_call(meta, arrays, group):
    split = arrays[0].shape[0]
    rows = split + arrays[2].shape[0]
    dtype = arrays[0].dtype
    return pl.pallas_call(
        functools.partial(pack_kernel, group=group),
        in_specs=[SMEM] + [pl.BlockSpec(memory_space=pltpu.HBM)] * 4,
        out_specs=[VMEM] * 3,
        out_shape=[jax.ShapeDtypeStruct((group // 2 * rows, 2 * HD), dtype)] * 2
        + [jax.ShapeDtypeStruct((split * group, 2 * HD), dtype)],
        scratch_shapes=[pltpu.SemaphoreType.DMA((6 * group,))],
        compiler_params=pltpu.CompilerParams(**PARAMS),
        cost_estimate=SMALL,
        name="pack",
    )(meta, *[pltpu.with_memory_space_constraint(a, pltpu.HBM) for a in arrays])


def regroup_kernel(*refs):
    sources, targets = refs[:-3], refs[-2:]
    rows = sources[0].shape[0] // 4
    size = rows * len(sources)
    for d in range(4):
        for n, source in enumerate(sources):
            low = d // 2 * size + n * rows
            targets[d % 2][low : low + rows, :] = source[d * rows : (d + 1) * rows, :]


def regroup_call(arrays, wait):
    rows, width = arrays[0].shape
    return pl.pallas_call(
        regroup_kernel,
        in_specs=[VMEM] * len(arrays) + [ANY],
        out_specs=[VMEM] * 2,
        out_shape=[jax.ShapeDtypeStruct((rows // 2 * len(arrays), width), arrays[0].dtype)] * 2,
        compiler_params=pltpu.CompilerParams(**PARAMS),
        cost_estimate=SMALL,
        name="regroup",
    )(*arrays, wait)


def pick_kernel(meta, source, wait, kept, given, sems):
    rows = source.shape[0]
    copies = []
    for d in range(4):
        at = pl.ds(pl.multiple_of((meta[0] ^ d) * WIDE, WIDE), WIDE)
        target = given if d % 2 else kept
        copies.append((source.at[:, at], target.at[pl.ds(d // 2 * rows, rows), :]))
    run_copies(copies, sems)


def pick_call(meta, array, wait):
    rows = array.shape[0]
    return pl.pallas_call(
        pick_kernel,
        in_specs=[SMEM, pl.BlockSpec(memory_space=pltpu.HBM), ANY],
        out_specs=[VMEM] * 2,
        out_shape=[jax.ShapeDtypeStruct((2 * rows, WIDE), array.dtype)] * 2,
        scratch_shapes=[pltpu.SemaphoreType.DMA((4,))],
        compiler_params=pltpu.CompilerParams(**PARAMS),
        cost_estimate=SMALL,
        name="pick",
    )(meta, pltpu.with_memory_space_constraint(array, pltpu.HBM), wait)


def turn_kernel(kept, came, *refs, pieces):
    near, onward = refs[-2:]
    size = kept.shape[0] // 2
    for start, part in pieces or [(0, size)]:
        for n, source in enumerate((kept, came)):
            at = 2 * start + n * part
            near[at : at + part, :] = source[start : start + part, :]
            onward[at : at + part, :] = source[size + start : size + start + part, :]


def turn_call(kept, came, *wait, pieces=()):
    return pl.pallas_call(
        functools.partial(turn_kernel, pieces=pieces),
        in_specs=[VMEM] * 2 + [ANY] * len(wait),
        out_specs=[VMEM] * 2,
        out_shape=[jax.ShapeDtypeStruct(kept.shape, kept.dtype)] * 2,
        compiler_params=pltpu.CompilerParams(**PARAMS),
        cost_estimate=SMALL,
        name="turn",
    )(kept, came, *wait)


def join_kernel(*refs, groups, count, waits):
    for n, spans in enumerate(groups):
        at = 0
        for source in refs[:count]:
            for low, high in spans:
                refs[count + waits + n][at : at + high - low, :] = source[low:high, :]
                at += high - low


def join_call(parts, *groups, wait=()):
    width, count = parts[0].shape[1], len(parts)
    return pl.pallas_call(
        functools.partial(join_kernel, groups=groups, count=count, waits=len(wait)),
        in_specs=[VMEM] * count + [ANY] * len(wait),
        out_specs=[VMEM] * len(groups),
        out_shape=[
            jax.ShapeDtypeStruct(
                (count * sum(high - low for low, high in spans), width), parts[0].dtype
            )
            for spans in groups
        ],
        compiler_params=pltpu.CompilerParams(**PARAMS),
        cost_estimate=SMALL,
        name="join",
    )(*parts, *wait)


def piece_of(rows, c):
    unit = rows // sum(PIECES)
    return sum(PIECES[:c]) * unit, PIECES[c] * unit


def share_of(half, n):
    unit = half // sum(SHARES)
    return sum(SHARES[:n]) * unit, SHARES[n] * unit


def weight_copies(meta, weight, targets, sems, fetch):
    copies = []
    half = weight.shape[1] // 2
    for n, (share, target) in enumerate(zip(fetch, targets)):
        start, width = share_of(half, share % len(SHARES))
        column = pl.multiple_of(meta[2 + share // len(SHARES)] + start, HD)
        for d in range(weight.shape[0] // WIDE):
            at = pl.ds(pl.multiple_of((meta[0] ^ d) * WIDE, WIDE), WIDE)
            copies.append(
                pltpu.make_async_copy(
                    weight.at[at, pl.ds(column, width)],
                    target.at[pl.ds(d * WIDE, WIDE), :],
                    sems.at[n, d],
                )
            )
    return copies


def attend_kernel(
    meta, lengths, *refs, kinds, group, rows, offset, has_state, piece, final, fetch, waits, scale
):
    refs = list(refs)
    q_ref = refs.pop(0)
    kv_refs = [refs.pop(0) for _ in kinds]
    if has_state:
        del refs[:2]
    if fetch:
        weight = refs.pop(0)
    del refs[:waits]
    out_refs = [refs.pop(0) for _ in range(final)]
    acc_ref, max_ref = refs.pop(0), refs.pop(0)
    heads = range(GROUP)
    pair = 2 * rows
    copies = []
    if fetch:
        copies = weight_copies(meta, weight, refs[:-1], refs[-1], fetch)
    for copy in copies:
        copy.start()

    def across(x, width):
        return x if width == HD else jnp.concatenate([x] * (width // HD), axis=1)

    def first_of(position, zero):
        start, found = jnp.int32(0), zero
        for r in range(lengths.shape[0]):
            found = jnp.where(start <= position, start, found)
            start = start + lengths[r]
        return found

    def row_block(i):
        start, part = piece_of(rows, i)
        size = 2 * part
        here = slice(2 * start, 2 * start + size)
        bases = [
            (meta[1] * group + (meta[0] ^ (offset + n))) * rows + start for n in range(2)
        ]
        lowest = jnp.minimum(*bases)
        highest = jnp.maximum(*bases) + part - 1

        def update(kv_ref, at, visible, fresh):
            keys = kv_ref[at, :HD]
            values = kv_ref[at, HD:]
            wide = jnp.concatenate([values, jnp.ones_like(values)], axis=1)
            if not fresh:
                old = [max_ref[h, here, :] for h in heads]
                kept = [acc_ref[h, here, :] for h in heads]
            tops, parts = [], []
            for h in heads:
                q = q_ref[here, h * HD : (h + 1) * HD]
                s = lax.dot_general(
                    q, keys, (((1,), (1,)), ((), ())), preferred_element_type=jnp.float32
                )
                if visible is not None:
                    s = jnp.where(visible, s, LOW)
                top = jnp.broadcast_to(jnp.max(s, axis=1, keepdims=True), (size, HD))
                if not fresh:
                    top = jnp.maximum(old[h], top)
                p = jnp.exp2((s - across(top, s.shape[1])) * scale).astype(jnp.bfloat16)
                term = jnp.dot(p, wide, preferred_element_type=jnp.float32)
                if not fresh:
                    term = kept[h] * across(jnp.exp2((old[h] - top) * scale), 2 * HD) + term
                tops.append(top)
                parts.append(term)
            for h in heads:
                acc_ref[h, here, :] = parts[h]
                max_ref[h, here, :] = tops[h]

        fresh = not has_state
        for kind, kv_ref in zip(kinds, kv_refs):
            if kind is None:
                for low in range(0, kv_ref.shape[0], 512):
                    update(kv_ref, slice(low, min(low + 512, kv_ref.shape[0])), None, fresh)
                    fresh = False
                continue
            first_low = first_of(lowest, jnp.int32(0))
            first_high = first_of(highest, jnp.int32(0))
            for j in range(group // 2):
                key_base = ((meta[1] - kind) * group + ((meta[0] ^ (2 * j)) & ~1)) * rows
                needed = (key_base <= highest) & (key_base + pair - 1 >= first_low)
                whole = (key_base + pair - 1 <= lowest) & (key_base >= first_high)
                at = slice(j * pair, (j + 1) * pair)

                @pl.when(needed & whole)
                def _(kv_ref=kv_ref, at=at):
                    update(kv_ref, at, None, False)

                @pl.when(needed & jnp.logical_not(whole))
                def _(kv_ref=kv_ref, at=at, key_base=key_base):
                    line = lax.broadcasted_iota(jnp.int32, (size, HD), 0)
                    position = line + jnp.where(line < part, bases[0], bases[1] - part)
                    first = first_of(position, jnp.zeros((size, HD), jnp.int32))
                    key_pos = key_base + (
                        lax.broadcasted_iota(jnp.int32, (size, pair), 1) ^ ((meta[0] & 1) * rows)
                    )
                    visible = (key_pos >= across(first, pair)) & (key_pos <= across(position, pair))
                    update(kv_ref, at, visible, False)

        for out_ref in out_refs:
            for h in heads:
                out_ref[:, h * HD : (h + 1) * HD] = (
                    acc_ref[h, here, :HD] / acc_ref[h, here, HD:]
                ).astype(jnp.bfloat16)

    for i in range(len(PIECES)) if piece is None else [piece]:
        row_block(i)
    for copy in copies:
        copy.wait()


def attend_call(
    meta, lengths, q, pieces, state, group, rows, offset, piece=None, final=False, weight=None, fetch=(), cost=None, wait=()
):
    kinds = tuple(kind for kind, _ in pieces)
    arrays = [array for _, array in pieces]
    operands = [meta, lengths, q] + arrays + list(state or ())
    out_shape = [
        jax.ShapeDtypeStruct((GROUP, q.shape[0], 2 * HD), jnp.float32),
        jax.ShapeDtypeStruct((GROUP, q.shape[0], HD), jnp.float32),
    ]
    in_specs = [SMEM, SMEM] + [VMEM] * (len(operands) - 2)
    aliases, scratch, done = {}, [], 0
    if final:
        done = 1
        size = 2 * piece_of(rows, piece)[1]
        out_shape = [jax.ShapeDtypeStruct((size, WIDE), jnp.bfloat16)] + out_shape
    if state is not None:
        aliases = {len(operands) - 2: done, len(operands) - 1: done + 1}
    if fetch:
        operands.append(pltpu.with_memory_space_constraint(weight, pltpu.HBM))
        in_specs.append(pl.BlockSpec(memory_space=pltpu.HBM))
        for share in fetch:
            width = share_of(weight.shape[1] // 2, share % len(SHARES))[1]
            out_shape.append(jax.ShapeDtypeStruct((weight.shape[0], width), weight.dtype))
        scratch = [pltpu.SemaphoreType.DMA((len(fetch), group))]
    operands += wait
    in_specs += [ANY] * len(wait)
    return pl.pallas_call(
        functools.partial(
            attend_kernel,
            kinds=kinds,
            group=group,
            rows=rows,
            offset=offset,
            has_state=state is not None,
            piece=piece,
            final=final,
            fetch=fetch,
            waits=len(wait),
            scale=HD**-0.5 * LOG2E,
        ),
        in_specs=in_specs,
        out_specs=[VMEM] * len(out_shape),
        out_shape=out_shape,
        scratch_shapes=scratch,
        input_output_aliases=aliases,
        compiler_params=pltpu.CompilerParams(**PARAMS),
        cost_estimate=cost or LARGE,
        name="attend",
    )(*operands)


def project_kernel(*refs, spans, count, waits, fetch):
    refs = list(refs)
    parts = [refs.pop(0) for _ in range(count)]
    weights = [refs.pop(0) for _ in range(len(spans) - len(fetch))]
    copies = []
    if fetch:
        *targets, sems = refs[-1 - len(fetch) :]
        copies = weight_copies(refs[0], refs[1], targets, sems, fetch)
        weights += targets
        refs = refs[2 : -1 - len(fetch)]
    outs = refs[waits:]
    for copy in copies:
        copy.start()
    lines = []
    for n in range(0, count, 3):
        near, other, far = parts[n : n + 3]
        size = near.shape[0] // 2
        lines.append(
            jnp.concatenate([near[:size], other[:size], far[:size], other[size:]], axis=1)
        )
    rows = jnp.concatenate(lines, axis=0) if len(lines) > 1 else lines[0]
    low = 0
    for k, (weight, (first, width)) in enumerate(zip(weights, spans)):
        n = k - (len(spans) - len(fetch))
        if n >= 0:
            each = len(copies) // len(fetch)
            for copy in copies[n * each : (n + 1) * each]:
                copy.wait()
        for at in range(0, width, TILE):
            wide = min(TILE, width - at)
            term = jnp.dot(
                rows, weight[:, first + at : first + at + wide], preferred_element_type=jnp.float32
            ).astype(jnp.bfloat16)
            top = 0
            for out in outs:
                out[:, low + at : low + at + wide] = term[top : top + out.shape[0]]
                top += out.shape[0]
        low += width


def project_call(parts, weights, spans, wait=(), meta=None, weight=None, fetch=()):
    width = sum(span[1] for span in spans)
    sizes = [part.shape[0] // 2 for part in parts[::3]]
    operands = [*parts, *weights]
    in_specs = [VMEM] * len(operands)
    scratch = []
    if fetch:
        operands += [meta, pltpu.with_memory_space_constraint(weight, pltpu.HBM)]
        in_specs += [SMEM, pl.BlockSpec(memory_space=pltpu.HBM)]
        scratch = [
            pltpu.VMEM((weight.shape[0], wide), weight.dtype) for _, wide in spans[-len(fetch) :]
        ] + [pltpu.SemaphoreType.DMA((len(fetch), weight.shape[0] // WIDE))]
    return pl.pallas_call(
        functools.partial(
            project_kernel, spans=tuple(spans), count=len(parts), waits=len(wait), fetch=fetch
        ),
        in_specs=in_specs + [ANY] * len(wait),
        out_specs=[VMEM] * len(sizes),
        out_shape=[jax.ShapeDtypeStruct((size, width), jnp.bfloat16) for size in sizes],
        scratch_shapes=scratch,
        compiler_params=pltpu.CompilerParams(**PARAMS),
        cost_estimate=SMALL,
        name="project",
    )(*operands, *wait)


def sum_kernel(*refs, counts):
    refs = list(refs)
    out = refs.pop()
    top = 0
    for count in counts:
        own = refs.pop(0)
        rows = slice(top, top + own.shape[0])
        top += own.shape[0]
        low = 0
        for _ in range(count):
            part = refs.pop(0)
            at = slice(low, low + part.shape[1])
            out[rows, at] = (own[:, at].astype(jnp.float32) + part[...].astype(jnp.float32)).astype(
                jnp.bfloat16
            )
            low += part.shape[1]


def sum_call(owns, came):
    operands = []
    for own, parts in zip(owns, came):
        operands += [own, *parts]
    rows = sum(own.shape[0] for own in owns)
    return pl.pallas_call(
        functools.partial(sum_kernel, counts=tuple(len(parts) for parts in came)),
        in_specs=[VMEM] * len(operands),
        out_specs=VMEM,
        out_shape=jax.ShapeDtypeStruct((rows, owns[0].shape[1]), jnp.bfloat16),
        compiler_params=pltpu.CompilerParams(**PARAMS),
        cost_estimate=SMALL,
        name="sum",
    )(*operands)


def per_device_planes(
    queries,
    prompt_keys,
    prompt_values,
    response_keys,
    response_values,
    lengths,
    out_weight,
    *,
    n_seq,
    n_tp,
):
    rows = queries.shape[0]
    group = prompt_keys.shape[1] // HD
    levels = n_seq // group
    seq = lax.axis_index("seq")
    me = lax.rem(seq, group)
    level = lax.div(seq, group)
    tp = lax.axis_index("tp")
    half = out_weight.shape[1] // n_tp
    meta = jnp.stack([me, level, (1 - tp) * half, tp * half]).astype(jnp.int32)

    def swap(x, d):
        return lax.ppermute(
            x, "seq", [(i, i - i % group + ((i % group) ^ d)) for i in range(n_seq)]
        )

    def shift(x, k, around):
        pairs = [(i, i + k * group) for i in range(n_seq)]
        if around:
            pairs = [(i, j % n_seq) for i, j in pairs]
        return lax.ppermute(x, "seq", [(i, j) for i, j in pairs if 0 <= j < n_seq])

    p_rows = prompt_keys.shape[0]
    kept, given, raw = pack_call(
        meta, [prompt_keys, prompt_values, response_keys, response_values], group
    )
    raws = [shift(raw, k, True) for k in range(1, levels)]
    close, onward = turn_call(kept, swap(given, 1))
    far_off = swap(onward, 2)
    size = p_rows + rows
    prompt, response = join_call(
        [close, far_off], ((0, p_rows), (size, size + p_rows)), ((p_rows, size), (size + p_rows, 2 * size))
    )

    def attend(q, offset, pieces, state, piece=None, final=False, fetch=(), cost=LARGE, wait=()):
        return attend_call(
            meta,
            lengths,
            q,
            pieces,
            state,
            group,
            rows,
            offset,
            piece,
            final,
            out_weight,
            fetch,
            cost,
            wait,
        )

    kept, given = pick_call(meta, queries, kept)
    q_near, onward = turn_call(kept, swap(given, 1), response, pieces=tuple(piece_of(rows, c) for c in range(len(PIECES))))
    q_far = swap(onward, 2)

    own_keys = [(None, prompt), (0, response)]
    back1 = shift(response, 1, False)
    near0, near1, *held = attend(q_near, 0, own_keys, None, fetch=(0, 1))
    near = [near0, near1]
    *far, share = attend(q_far, 2, own_keys, None, cost=SMALL, fetch=(2,), wait=near[1:])
    held.append(share)
    kept, given = regroup_call(raws, far[1])
    others0, onward = turn_call(kept, swap(given, 1))
    others1 = swap(onward, 2)
    back2 = shift(back1, 1, False)
    early, late = [(1, back1), (None, others0)], [(None, others1), (2, back2)]

    def project(part, low, high, wait=()):
        used = []
        for n in range(len(SHARES)):
            start, width = share_of(half, n)
            span = max(low - start, 0), min(high - start, width)
            if span[0] < span[1]:
                used.append((held[n], (span[0], span[1] - span[0])))
        (term,) = project_call(part, [a for a, _ in used], [b for _, b in used], wait)
        return term

    def cross(term):
        return lax.ppermute(term, "tp", [(0, 1), (1, 0)])

    def bring(near_done, far_done, *wait):
        came = swap(far_done, 2)
        (give,) = join_call([near_done, came], ((near_done.shape[0] // 2, near_done.shape[0]),), wait=wait)
        return [near_done, swap(give, 1), came]

    *near, share = attend(q_near, 0, early, near, piece=0, fetch=(3,))
    held.append(share)
    *far, share = attend(q_far, 2, early, far, piece=0, fetch=(4,), cost=SMALL, wait=near[1:])
    held.append(share)
    far_done, *far = attend(q_far, 2, late, far, piece=0, final=True, cost=SMALL)
    near_done, *near = attend(q_near, 0, late, near, piece=0, final=True, wait=[far_done])
    far = attend(q_far, 2, early, far, piece=1, cost=SMALL, wait=[near_done])
    part0 = bring(near_done, far_done, far[1])
    terms = [project(part0, 0, half, far[1:])]
    came0 = [cross(term) for term in terms]

    far_done, *far = attend(q_far, 2, late, far, piece=1, final=True, wait=terms)
    near_done, *near, share = attend(
        q_near, 0, early + late, near, piece=1, final=True, fetch=(5,), wait=[far_done]
    )
    held.append(share)
    part1 = bring(near_done, far_done, near[1])
    terms = [project(part1, 0, half // 2)]
    terms.append(project(part1, half // 2, half, [came0[0], terms[0]]))
    came1 = [cross(term) for term in terms]
    came = [came0, came1]
    own = project_call(
        part0 + part1,
        held[len(SHARES) :],
        [(0, share_of(half, n)[1]) for n in range(len(SHARES))],
        terms[1:],
        meta,
        out_weight,
        (6, 7),
    )
    return sum_call(own, came)


def solution(mesh):
    in_specs = (
        P("seq", "tp"),
        P("seq", "tp"),
        P("seq", "tp"),
        P("seq", "tp"),
        P("seq", "tp"),
        P(),
        P("tp", None),
    )
    out_specs = P("seq", "tp")
    n_seq, n_tp = mesh.shape["seq"], mesh.shape["tp"]
    if n_tp == 2 and n_seq == 16:
        body = functools.partial(per_device_planes, n_seq=n_seq, n_tp=n_tp)
    else:
        body = per_device_general
    return jax.shard_map(body, mesh=mesh, in_specs=in_specs, out_specs=out_specs, check_vma=False)
```

```python
import functools

import jax
import jax.numpy as jnp
from jax import lax
from jax.experimental import pallas as pl
from jax.experimental.pallas import tpu as pltpu
from jax.sharding import PartitionSpec as P

HEADS = 40
KVH = 8
HD = 128
GROUP = HEADS // KVH
WIDE = GROUP * HD
LOG2E = 1.4426950408889634
LOW = -1e30
PIECES = (5, 3)
SHARES = (3, 2, 3, 2)
TILE = 256
ANY = pl.BlockSpec(memory_space=pl.ANY)
VMEM = pl.BlockSpec(memory_space=pltpu.VMEM)
SMEM = pl.BlockSpec(memory_space=pltpu.SMEM)
SMALL = pl.CostEstimate(flops=1000, bytes_accessed=1000, transcendentals=0)
LARGE = pl.CostEstimate(flops=2 * 10**10, bytes_accessed=1000, transcendentals=0)
FIRST = pl.CostEstimate(flops=2 * 10**10, bytes_accessed=1000, transcendentals=0)
PARAMS = dict(vmem_limit_bytes=16 * 2**20)


def segment_layout(lengths, first_row, row_count):
    positions = first_row + jnp.arange(row_count, dtype=jnp.int32)
    seg_ends = jnp.cumsum(lengths)
    seg_starts = seg_ends - lengths
    inside = (positions[:, None] >= seg_starts[None, :]) & (positions[:, None] < seg_ends[None, :])
    own_start = jnp.sum(jnp.where(inside, seg_starts[None, :], 0), axis=1)
    return (positions, own_start)


def update_state(running, grouped, key_block, value_block, visible, scale_factor):
    maximum, summed, weighted = running
    scores = (
        jnp.einsum("rkgd,nkd->rkgn", grouped, key_block, preferred_element_type=jnp.float32)
        * scale_factor
    )
    if visible is not None:
        scores = jnp.where(visible[:, None, None, :], scores, -jnp.inf)
    new_max = jnp.maximum(maximum, jnp.max(scores, axis=3))
    weights = jnp.exp(scores - new_max[..., None])
    rescale = jnp.exp(maximum - new_max)
    rounded = weights.astype(jnp.bfloat16)
    summed = summed * rescale + jnp.sum(weights, axis=3)
    weighted = weighted * rescale[..., None] + jnp.einsum(
        "rkgn,nkd->rkgd", rounded, value_block, preferred_element_type=jnp.float32
    )
    return (new_max, summed, weighted)


def per_device_general(
    queries, prompt_keys, prompt_values, response_keys, response_values, lengths, out_weight
):
    row_count = queries.shape[0]
    kv_local = prompt_keys.shape[1] // HD
    scale_factor = HD ** (-0.5)
    grouped = queries.reshape(row_count, kv_local, GROUP, HD)
    first_row = lax.axis_index("seq") * row_count
    positions, own_start = segment_layout(lengths, first_row, row_count)
    softmax_state = (
        jnp.full((row_count, kv_local, GROUP), -jnp.inf, jnp.float32),
        jnp.zeros((row_count, kv_local, GROUP), jnp.float32),
        jnp.zeros((row_count, kv_local, GROUP, HD), jnp.float32),
    )
    prompt_pair = jnp.stack([prompt_keys, prompt_values])
    fragment = lax.all_gather(prompt_pair, "seq", axis=1, tiled=True)
    frag_rows = fragment.shape[1]
    key_block = fragment[0].reshape(frag_rows, kv_local, HD)
    value_block = fragment[1].reshape(frag_rows, kv_local, HD)
    softmax_state = update_state(softmax_state, grouped, key_block, value_block, None, scale_factor)
    response_pair = jnp.stack([response_keys, response_values])
    fragment = lax.all_gather(response_pair, "seq", axis=1, tiled=True)
    frag_rows = fragment.shape[1]
    key_pos = jnp.arange(frag_rows, dtype=jnp.int32)
    visible = (key_pos[None, :] <= positions[:, None]) & (key_pos[None, :] >= own_start[:, None])
    key_block = fragment[0].reshape(frag_rows, kv_local, HD)
    value_block = fragment[1].reshape(frag_rows, kv_local, HD)
    softmax_state = update_state(
        softmax_state, grouped, key_block, value_block, visible, scale_factor
    )
    maximum, summed, weighted = softmax_state
    attended = (
        (weighted / summed[..., None])
        .astype(jnp.bfloat16)
        .reshape(row_count, kv_local * GROUP * HD)
    )
    partial_out = jnp.dot(attended, out_weight, preferred_element_type=jnp.float32)
    return lax.psum_scatter(partial_out.astype(jnp.bfloat16), "tp", scatter_dimension=1, tiled=True)


def pack_kernel(meta, *refs, group):
    sources, (kept, given, raw, sems) = refs[:4], refs[4:]
    split = sources[0].shape[0]
    size = split + sources[2].shape[0]
    copies = []
    for d in range(group):
        at = pl.ds(pl.multiple_of((meta[0] ^ d) * HD, HD), HD)
        target = given if d % 2 else kept
        for n, source in enumerate(sources):
            side = pl.ds((n % 2) * HD, HD)
            rows = pl.ds(d // 2 * size + (0 if n < 2 else split), source.shape[0])
            copies.append((source.at[:, at], target.at[rows, side]))
            if n < 2:
                copies.append((source.at[:, at], raw.at[pl.ds(d * split, split), side]))
    run_copies(copies, sems)


def run_copies(copies, sems):
    started = [
        pltpu.make_async_copy(source, target, sems.at[n])
        for n, (source, target) in enumerate(copies)
    ]
    for copy in started:
        copy.start()
    for copy in started:
        copy.wait()


def pack_call(meta, arrays, group):
    split = arrays[0].shape[0]
    rows = split + arrays[2].shape[0]
    dtype = arrays[0].dtype
    return pl.pallas_call(
        functools.partial(pack_kernel, group=group),
        in_specs=[SMEM] + [pl.BlockSpec(memory_space=pltpu.HBM)] * 4,
        out_specs=[VMEM] * 3,
        out_shape=[jax.ShapeDtypeStruct((group // 2 * rows, 2 * HD), dtype)] * 2
        + [jax.ShapeDtypeStruct((split * group, 2 * HD), dtype)],
        scratch_shapes=[pltpu.SemaphoreType.DMA((6 * group,))],
        compiler_params=pltpu.CompilerParams(**PARAMS),
        cost_estimate=SMALL,
        name="pack",
    )(meta, *[pltpu.with_memory_space_constraint(a, pltpu.HBM) for a in arrays])


def regroup_kernel(*refs):
    sources, targets = refs[:-3], refs[-2:]
    rows = sources[0].shape[0] // 4
    size = rows * len(sources)
    for d in range(4):
        for n, source in enumerate(sources):
            low = d // 2 * size + n * rows
            targets[d % 2][low : low + rows, :] = source[d * rows : (d + 1) * rows, :]


def regroup_call(arrays, wait):
    rows, width = arrays[0].shape
    return pl.pallas_call(
        regroup_kernel,
        in_specs=[VMEM] * len(arrays) + [ANY],
        out_specs=[VMEM] * 2,
        out_shape=[jax.ShapeDtypeStruct((rows // 2 * len(arrays), width), arrays[0].dtype)] * 2,
        compiler_params=pltpu.CompilerParams(**PARAMS),
        cost_estimate=SMALL,
        name="regroup",
    )(*arrays, wait)


def pick_kernel(meta, source, wait, kept, given, sems):
    rows = source.shape[0]
    copies = []
    for d in range(4):
        at = pl.ds(pl.multiple_of((meta[0] ^ d) * WIDE, WIDE), WIDE)
        target = given if d % 2 else kept
        copies.append((source.at[:, at], target.at[pl.ds(d // 2 * rows, rows), :]))
    run_copies(copies, sems)


def pick_call(meta, array, wait):
    rows = array.shape[0]
    return pl.pallas_call(
        pick_kernel,
        in_specs=[SMEM, pl.BlockSpec(memory_space=pltpu.HBM), ANY],
        out_specs=[VMEM] * 2,
        out_shape=[jax.ShapeDtypeStruct((2 * rows, WIDE), array.dtype)] * 2,
        scratch_shapes=[pltpu.SemaphoreType.DMA((4,))],
        compiler_params=pltpu.CompilerParams(**PARAMS),
        cost_estimate=SMALL,
        name="pick",
    )(meta, pltpu.with_memory_space_constraint(array, pltpu.HBM), wait)


def turn_kernel(kept, came, *refs, pieces):
    near, onward = refs[-2:]
    size = kept.shape[0] // 2
    for start, part in pieces or [(0, size)]:
        for n, source in enumerate((kept, came)):
            at = 2 * start + n * part
            near[at : at + part, :] = source[start : start + part, :]
            onward[at : at + part, :] = source[size + start : size + start + part, :]


def turn_call(kept, came, *wait, pieces=()):
    return pl.pallas_call(
        functools.partial(turn_kernel, pieces=pieces),
        in_specs=[VMEM] * 2 + [ANY] * len(wait),
        out_specs=[VMEM] * 2,
        out_shape=[jax.ShapeDtypeStruct(kept.shape, kept.dtype)] * 2,
        compiler_params=pltpu.CompilerParams(**PARAMS),
        cost_estimate=SMALL,
        name="turn",
    )(kept, came, *wait)


def join_kernel(*refs, groups, count, waits):
    for n, spans in enumerate(groups):
        at = 0
        for source in refs[:count]:
            for low, high in spans:
                refs[count + waits + n][at : at + high - low, :] = source[low:high, :]
                at += high - low


def join_call(parts, *groups, wait=()):
    width, count = parts[0].shape[1], len(parts)
    return pl.pallas_call(
        functools.partial(join_kernel, groups=groups, count=count, waits=len(wait)),
        in_specs=[VMEM] * count + [ANY] * len(wait),
        out_specs=[VMEM] * len(groups),
        out_shape=[
            jax.ShapeDtypeStruct(
                (count * sum(high - low for low, high in spans), width), parts[0].dtype
            )
            for spans in groups
        ],
        compiler_params=pltpu.CompilerParams(**PARAMS),
        cost_estimate=SMALL,
        name="join",
    )(*parts, *wait)


def piece_of(rows, c):
    unit = rows // sum(PIECES)
    return sum(PIECES[:c]) * unit, PIECES[c] * unit


def share_of(half, n):
    unit = half // sum(SHARES)
    return sum(SHARES[:n]) * unit, SHARES[n] * unit


def weight_copies(meta, weight, targets, sems, fetch):
    copies = []
    half = weight.shape[1] // 2
    for n, (share, target) in enumerate(zip(fetch, targets)):
        start, width = share_of(half, share % len(SHARES))
        column = pl.multiple_of(meta[2 + share // len(SHARES)] + start, HD)
        for d in range(weight.shape[0] // WIDE):
            at = pl.ds(pl.multiple_of((meta[0] ^ d) * WIDE, WIDE), WIDE)
            copies.append(
                pltpu.make_async_copy(
                    weight.at[at, pl.ds(column, width)],
                    target.at[pl.ds(d * WIDE, WIDE), :],
                    sems.at[n, d],
                )
            )
    return copies


def attend_kernel(
    meta, lengths, *refs, kinds, group, rows, offset, has_state, piece, final, fetch, waits, scale
):
    refs = list(refs)
    q_ref = refs.pop(0)
    kv_refs = [refs.pop(0) for _ in kinds]
    if has_state:
        del refs[:2]
    if fetch:
        weight = refs.pop(0)
    del refs[:waits]
    out_refs = [refs.pop(0) for _ in range(final)]
    acc_ref, max_ref = refs.pop(0), refs.pop(0)
    heads = range(GROUP)
    pair = 2 * rows
    copies = []
    if fetch:
        copies = weight_copies(meta, weight, refs[:-1], refs[-1], fetch)
    for copy in copies:
        copy.start()

    def across(x, width):
        return x if width == HD else jnp.concatenate([x] * (width // HD), axis=1)

    def first_of(position, zero):
        start, found = jnp.int32(0), zero
        for r in range(lengths.shape[0]):
            found = jnp.where(start <= position, start, found)
            start = start + lengths[r]
        return found

    def row_block(i):
        start, part = piece_of(rows, i)
        size = 2 * part
        here = slice(2 * start, 2 * start + size)
        bases = [
            (meta[1] * group + (meta[0] ^ (offset + n))) * rows + start for n in range(2)
        ]
        lowest = jnp.minimum(*bases)
        highest = jnp.maximum(*bases) + part - 1

        def update(kv_ref, at, visible, fresh):
            keys = kv_ref[at, :HD]
            values = kv_ref[at, HD:]
            wide = jnp.concatenate([values, jnp.ones_like(values)], axis=1)
            if not fresh:
                old = [max_ref[h, here, :] for h in heads]
                kept = [acc_ref[h, here, :] for h in heads]
            tops, parts = [], []
            for h in heads:
                q = q_ref[here, h * HD : (h + 1) * HD]
                s = lax.dot_general(
                    q, keys, (((1,), (1,)), ((), ())), preferred_element_type=jnp.float32
                )
                if visible is not None:
                    s = jnp.where(visible, s, LOW)
                top = jnp.broadcast_to(jnp.max(s, axis=1, keepdims=True), (size, HD))
                if not fresh:
                    top = jnp.maximum(old[h], top)
                p = jnp.exp2((s - across(top, s.shape[1])) * scale).astype(jnp.bfloat16)
                term = jnp.dot(p, wide, preferred_element_type=jnp.float32)
                if not fresh:
                    term = kept[h] * across(jnp.exp2((old[h] - top) * scale), 2 * HD) + term
                tops.append(top)
                parts.append(term)
            for h in heads:
                acc_ref[h, here, :] = parts[h]
                max_ref[h, here, :] = tops[h]

        fresh = not has_state
        for kind, kv_ref in zip(kinds, kv_refs):
            if kind is None:
                for low in range(0, kv_ref.shape[0], 512):
                    update(kv_ref, slice(low, min(low + 512, kv_ref.shape[0])), None, fresh)
                    fresh = False
                continue
            first_low = first_of(lowest, jnp.int32(0))
            first_high = first_of(highest, jnp.int32(0))
            for j in range(group // 2):
                key_base = ((meta[1] - kind) * group + ((meta[0] ^ (2 * j)) & ~1)) * rows
                needed = (key_base <= highest) & (key_base + pair - 1 >= first_low)
                whole = (key_base + pair - 1 <= lowest) & (key_base >= first_high)
                at = slice(j * pair, (j + 1) * pair)

                @pl.when(needed & whole)
                def _(kv_ref=kv_ref, at=at):
                    update(kv_ref, at, None, False)

                @pl.when(needed & jnp.logical_not(whole))
                def _(kv_ref=kv_ref, at=at, key_base=key_base):
                    line = lax.broadcasted_iota(jnp.int32, (size, HD), 0)
                    position = line + jnp.where(line < part, bases[0], bases[1] - part)
                    first = first_of(position, jnp.zeros((size, HD), jnp.int32))
                    key_pos = key_base + (
                        lax.broadcasted_iota(jnp.int32, (size, pair), 1) ^ ((meta[0] & 1) * rows)
                    )
                    visible = (key_pos >= across(first, pair)) & (key_pos <= across(position, pair))
                    update(kv_ref, at, visible, False)

        for out_ref in out_refs:
            for h in heads:
                out_ref[:, h * HD : (h + 1) * HD] = (
                    acc_ref[h, here, :HD] / acc_ref[h, here, HD:]
                ).astype(jnp.bfloat16)

    for i in range(len(PIECES)) if piece is None else [piece]:
        row_block(i)
    for copy in copies:
        copy.wait()


def attend_call(
    meta, lengths, q, pieces, state, group, rows, offset, piece=None, final=False, weight=None, fetch=(), cost=None, wait=()
):
    kinds = tuple(kind for kind, _ in pieces)
    arrays = [array for _, array in pieces]
    operands = [meta, lengths, q] + arrays + list(state or ())
    out_shape = [
        jax.ShapeDtypeStruct((GROUP, q.shape[0], 2 * HD), jnp.float32),
        jax.ShapeDtypeStruct((GROUP, q.shape[0], HD), jnp.float32),
    ]
    in_specs = [SMEM, SMEM] + [VMEM] * (len(operands) - 2)
    aliases, scratch, done = {}, [], 0
    if final:
        done = 1
        size = 2 * piece_of(rows, piece)[1]
        out_shape = [jax.ShapeDtypeStruct((size, WIDE), jnp.bfloat16)] + out_shape
    if state is not None:
        aliases = {len(operands) - 2: done, len(operands) - 1: done + 1}
    if fetch:
        operands.append(pltpu.with_memory_space_constraint(weight, pltpu.HBM))
        in_specs.append(pl.BlockSpec(memory_space=pltpu.HBM))
        for share in fetch:
            width = share_of(weight.shape[1] // 2, share % len(SHARES))[1]
            out_shape.append(jax.ShapeDtypeStruct((weight.shape[0], width), weight.dtype))
        scratch = [pltpu.SemaphoreType.DMA((len(fetch), group))]
    operands += wait
    in_specs += [ANY] * len(wait)
    return pl.pallas_call(
        functools.partial(
            attend_kernel,
            kinds=kinds,
            group=group,
            rows=rows,
            offset=offset,
            has_state=state is not None,
            piece=piece,
            final=final,
            fetch=fetch,
            waits=len(wait),
            scale=HD**-0.5 * LOG2E,
        ),
        in_specs=in_specs,
        out_specs=[VMEM] * len(out_shape),
        out_shape=out_shape,
        scratch_shapes=scratch,
        input_output_aliases=aliases,
        compiler_params=pltpu.CompilerParams(**PARAMS),
        cost_estimate=cost or LARGE,
        name="attend",
    )(*operands)


def project_kernel(*refs, spans, count, waits, fetch):
    refs = list(refs)
    parts = [refs.pop(0) for _ in range(count)]
    weights = [refs.pop(0) for _ in range(len(spans) - len(fetch))]
    copies = []
    if fetch:
        *targets, sems = refs[-1 - len(fetch) :]
        copies = weight_copies(refs[0], refs[1], targets, sems, fetch)
        weights += targets
        refs = refs[2 : -1 - len(fetch)]
    outs = refs[waits:]
    for copy in copies:
        copy.start()
    lines = []
    for n in range(0, count, 3):
        near, other, far = parts[n : n + 3]
        size = near.shape[0] // 2
        lines.append(
            jnp.concatenate([near[:size], other[:size], far[:size], other[size:]], axis=1)
        )
    rows = jnp.concatenate(lines, axis=0) if len(lines) > 1 else lines[0]
    low = 0
    for k, (weight, (first, width)) in enumerate(zip(weights, spans)):
        n = k - (len(spans) - len(fetch))
        if n >= 0:
            each = len(copies) // len(fetch)
            for copy in copies[n * each : (n + 1) * each]:
                copy.wait()
        for at in range(0, width, TILE):
            wide = min(TILE, width - at)
            term = jnp.dot(
                rows, weight[:, first + at : first + at + wide], preferred_element_type=jnp.float32
            ).astype(jnp.bfloat16)
            top = 0
            for out in outs:
                out[:, low + at : low + at + wide] = term[top : top + out.shape[0]]
                top += out.shape[0]
        low += width


def project_call(parts, weights, spans, wait=(), meta=None, weight=None, fetch=()):
    width = sum(span[1] for span in spans)
    sizes = [part.shape[0] // 2 for part in parts[::3]]
    operands = [*parts, *weights]
    in_specs = [VMEM] * len(operands)
    scratch = []
    if fetch:
        operands += [meta, pltpu.with_memory_space_constraint(weight, pltpu.HBM)]
        in_specs += [SMEM, pl.BlockSpec(memory_space=pltpu.HBM)]
        scratch = [
            pltpu.VMEM((weight.shape[0], wide), weight.dtype) for _, wide in spans[-len(fetch) :]
        ] + [pltpu.SemaphoreType.DMA((len(fetch), weight.shape[0] // WIDE))]
    return pl.pallas_call(
        functools.partial(
            project_kernel, spans=tuple(spans), count=len(parts), waits=len(wait), fetch=fetch
        ),
        in_specs=in_specs + [ANY] * len(wait),
        out_specs=[VMEM] * len(sizes),
        out_shape=[jax.ShapeDtypeStruct((size, width), jnp.bfloat16) for size in sizes],
        scratch_shapes=scratch,
        compiler_params=pltpu.CompilerParams(**PARAMS),
        cost_estimate=SMALL,
        name="project",
    )(*operands, *wait)


def sum_kernel(*refs, counts):
    refs = list(refs)
    out = refs.pop()
    top = 0
    for count in counts:
        own = refs.pop(0)
        rows = slice(top, top + own.shape[0])
        top += own.shape[0]
        low = 0
        for _ in range(count):
            part = refs.pop(0)
            at = slice(low, low + part.shape[1])
            out[rows, at] = (own[:, at].astype(jnp.float32) + part[...].astype(jnp.float32)).astype(
                jnp.bfloat16
            )
            low += part.shape[1]


def sum_call(owns, came):
    operands = []
    for own, parts in zip(owns, came):
        operands += [own, *parts]
    rows = sum(own.shape[0] for own in owns)
    return pl.pallas_call(
        functools.partial(sum_kernel, counts=tuple(len(parts) for parts in came)),
        in_specs=[VMEM] * len(operands),
        out_specs=VMEM,
        out_shape=jax.ShapeDtypeStruct((rows, owns[0].shape[1]), jnp.bfloat16),
        compiler_params=pltpu.CompilerParams(**PARAMS),
        cost_estimate=SMALL,
        name="sum",
    )(*operands)


def per_device_planes(
    queries,
    prompt_keys,
    prompt_values,
    response_keys,
    response_values,
    lengths,
    out_weight,
    *,
    n_seq,
    n_tp,
):
    rows = queries.shape[0]
    group = prompt_keys.shape[1] // HD
    levels = n_seq // group
    seq = lax.axis_index("seq")
    me = lax.rem(seq, group)
    level = lax.div(seq, group)
    tp = lax.axis_index("tp")
    half = out_weight.shape[1] // n_tp
    meta = jnp.stack([me, level, (1 - tp) * half, tp * half]).astype(jnp.int32)

    def swap(x, d):
        return lax.ppermute(
            x, "seq", [(i, i - i % group + ((i % group) ^ d)) for i in range(n_seq)]
        )

    def shift(x, k, around):
        pairs = [(i, i + k * group) for i in range(n_seq)]
        if around:
            pairs = [(i, j % n_seq) for i, j in pairs]
        return lax.ppermute(x, "seq", [(i, j) for i, j in pairs if 0 <= j < n_seq])

    p_rows = prompt_keys.shape[0]
    kept, given, raw = pack_call(
        meta, [prompt_keys, prompt_values, response_keys, response_values], group
    )
    raws = [shift(raw, k, True) for k in range(1, levels)]
    close, onward = turn_call(kept, swap(given, 1))
    far_off = swap(onward, 2)
    def attend(q, offset, pieces, state, piece=None, final=False, fetch=(), cost=LARGE, wait=()):
        return attend_call(
            meta,
            lengths,
            q,
            pieces,
            state,
            group,
            rows,
            offset,
            piece,
            final,
            out_weight,
            fetch,
            cost,
            wait,
        )

    kept, given = pick_call(meta, queries, kept)
    q_near, onward = turn_call(kept, swap(given, 1), far_off, pieces=tuple(piece_of(rows, c) for c in range(len(PIECES))))
    q_far = swap(onward, 2)
    size = p_rows + rows
    prompt, response = join_call(
        [close, far_off], ((0, p_rows), (size, size + p_rows)), ((p_rows, size), (size + p_rows, 2 * size)),
        wait=[onward],
    )

    own_keys = [(None, prompt), (0, response)]
    back1 = shift(response, 1, False)
    near0, near1, *held = attend(q_near, 0, own_keys, None, fetch=(0, 1))
    near = [near0, near1]
    *far, share = attend(q_far, 2, own_keys, None, cost=SMALL, fetch=(2,), wait=near[1:])
    held.append(share)
    kept, given = regroup_call(raws, far[1])
    others0, onward = turn_call(kept, swap(given, 1))
    others1 = swap(onward, 2)
    back2 = shift(back1, 1, False)
    early, late = [(1, back1), (None, others0)], [(None, others1), (2, back2)]

    def project(part, low, high, wait=()):
        used = []
        for n in range(len(SHARES)):
            start, width = share_of(half, n)
            span = max(low - start, 0), min(high - start, width)
            if span[0] < span[1]:
                used.append((held[n], (span[0], span[1] - span[0])))
        (term,) = project_call(part, [a for a, _ in used], [b for _, b in used], wait)
        return term

    def cross(term):
        return lax.ppermute(term, "tp", [(0, 1), (1, 0)])

    def bring(near_done, far_done, *wait):
        came = swap(far_done, 2)
        (give,) = join_call([near_done, came], ((near_done.shape[0] // 2, near_done.shape[0]),), wait=wait)
        return [near_done, swap(give, 1), came]

    *near, share = attend(q_near, 0, early, near, piece=0, fetch=(3,))
    held.append(share)
    *far, share = attend(q_far, 2, early, far, piece=0, fetch=(4,), cost=SMALL, wait=near[1:])
    held.append(share)
    far_done, *far = attend(q_far, 2, late, far, piece=0, final=True, cost=SMALL)
    near_done, *near = attend(q_near, 0, late, near, piece=0, final=True, wait=[far_done])
    far = attend(q_far, 2, early, far, piece=1, cost=SMALL, wait=[near_done])
    part0 = bring(near_done, far_done, far[1])
    terms = [project(part0, 0, half, far[1:])]
    came0 = [cross(term) for term in terms]

    far_done, *far = attend(q_far, 2, late, far, piece=1, final=True, wait=terms)
    near_done, *near, share = attend(
        q_near, 0, early + late, near, piece=1, final=True, fetch=(5,), wait=[far_done]
    )
    held.append(share)
    part1 = bring(near_done, far_done, near[1])
    terms = [project(part1, 0, half // 2)]
    terms.append(project(part1, half // 2, half, [came0[0], terms[0]]))
    came1 = [cross(term) for term in terms]
    came = [came0, came1]
    own = project_call(
        part0 + part1,
        held[len(SHARES) :],
        [(0, share_of(half, n)[1]) for n in range(len(SHARES))],
        terms[1:],
        meta,
        out_weight,
        (6, 7),
    )
    return sum_call(own, came)


def solution(mesh):
    in_specs = (
        P("seq", "tp"),
        P("seq", "tp"),
        P("seq", "tp"),
        P("seq", "tp"),
        P("seq", "tp"),
        P(),
        P("tp", None),
    )
    out_specs = P("seq", "tp")
    n_seq, n_tp = mesh.shape["seq"], mesh.shape["tp"]
    if n_tp == 2 and n_seq == 16:
        body = functools.partial(per_device_planes, n_seq=n_seq, n_tp=n_tp)
    else:
        body = per_device_general
    return jax.shard_map(body, mesh=mesh, in_specs=in_specs, out_specs=out_specs, check_vma=False)
```
